256 devices in a mesh: context: 32 (over z, x), tensor: 8 (over y, core).
Axes of the slice: x: 4, y: 4, z: 8, core: 2. Of those that a mesh axis runs over, the one named last changes fastest.
Arguments:
- activations: bfloat16 [16384, 3072], P(('context', 'tensor')), may hold values from -6 to 6
- w_qkv: bfloat16 [3072, 3, 4096], P(None, None, 'tensor'), may hold values from -0.109375 to 0.109375
- w_out: bfloat16 [4096, 3072], P('tensor'), may hold values from -0.09375 to 0.09375
- log_decay: float32 [32, 16384], P('tensor', 'context'), may hold values from -0.7 to 0
Outputs:
- mixed: bfloat16 [16384, 3072], P(('context', 'tensor'))
The draws below stay inside these ranges and needn't reach their ends.
All inputs are finite; a program needn't handle non-finite values.
Results may differ from the reference program's by a relative error of at most 0.02.
Values may be sent and summed in bfloat16 or wider, within the bound.
A program may use at most 128 MiB of HBM per device.

```python
import math
import jax
import jax.numpy as jnp
from jax import lax

D = 3072
HEADS = 32
HEAD_DIM = 128
BLOCK = 256
TOKENS = 16384
N_TENSOR = 8


def draw_log_decay(key, part):
    key = jax.random.fold_in(key, 7)
    keys = jax.random.split(key, 8)
    slow_share = 0.5
    medium_fraction = 0.25
    choose = jax.random.uniform(keys[0], (HEADS, 1), jnp.float32, 0.0, 1.0)
    slow = choose < slow_share
    medium = jnp.logical_and(choose >= slow_share, choose < slow_share + medium_fraction)
    slow_rate = jnp.exp(jax.random.uniform(keys[1], (HEADS, 1), jnp.float32, math.log(0.1), math.log(0.5))) / TOKENS
    medium_rate = jnp.exp(jax.random.uniform(keys[7], (HEADS, 1), jnp.float32, math.log(1.0 / 16.0), math.log(1.0 / 4.0))) / BLOCK
    fast_rate = jnp.exp(jax.random.uniform(keys[2], (HEADS, 1), jnp.float32, math.log(1.0 / 50.0), math.log(1.0 / 30.0)))
    rate = jnp.where(slow, slow_rate, jnp.where(medium, medium_rate, fast_rate))
    spread = jnp.exp(jax.random.uniform(keys[3], (HEADS, TOKENS // BLOCK), jnp.float32, math.log(0.5), math.log(2.0)))
    spread = jnp.repeat(spread, BLOCK, axis=1)
    rough = jax.random.uniform(keys[4], (HEADS, TOKENS), jnp.float32, 0.5, 1.5)
    gentle_multiplier = -rate * spread * rough
    probe_locations = jax.random.randint(keys[5], (HEADS, 2), 0, TOKENS)
    sequence_offsets = jnp.arange(TOKENS)
    spike_multiplier = jnp.any(sequence_offsets[None, :, None] == probe_locations[:, None, :], axis=2)
    retained_coefficients = jax.random.uniform(keys[6], (HEADS, TOKENS), jnp.float32, 0.5, 0.8)
    return jnp.where(spike_multiplier, jnp.log(retained_coefficients), gentle_multiplier).astype(jnp.float32)


def level_of(rng, shape, cuts, low, largest):
    def one(position, blocks):
        draws = jax.random.uniform(jax.random.fold_in(jax.random.fold_in(rng, 6), position), (blocks,), jnp.float32, low / len(cuts), largest / len(cuts))
        return jnp.repeat(jnp.exp(draws), shape[position] // blocks).reshape((-1,) + (1,) * (len(shape) - position - 1))

    factor_of = one(*cuts[0])
    for cut in cuts[1:]:
        factor_of = factor_of * one(*cut)
    return factor_of


def noise(key, dims, deviation, most, cuts=(), kind=jnp.bfloat16):
    result = jax.random.normal(key, dims, jnp.float32) * deviation
    if len(cuts) > 0:
        result = level_of(key, dims, cuts, -0.22, 0.18) * result
    return jnp.clip(result, min=-most, max=most).astype(kind)


def setup_inputs(seed: int = 0) -> dict:
    seeds = jax.random.split(jax.random.key(seed), 5)
    activations = noise(seeds[0], (TOKENS, D), 1.0, 6.0, ((0, 256),))
    w_qkv = noise(seeds[1], (D, 3, HEADS * HEAD_DIM), D ** -0.5, 0.109375, ((2, 8),))
    w_out = noise(seeds[2], (HEADS * HEAD_DIM, D), (HEADS * HEAD_DIM) ** -0.5, 0.09375, ((0, 8),))
    log_decay = draw_log_decay(jax.random.fold_in(seeds[4], 71), 0)
    return {"activations": activations, "w_qkv": w_qkv, "w_out": w_out, "log_decay": log_decay}


def block_step(state, items):
    queries, keys, values, decay = items
    cumulative = jnp.cumsum(decay, axis=1)
    size = decay.shape[1]
    lower = jnp.arange(size)[:, None] >= jnp.arange(size)[None, :]
    gaps = jnp.minimum(cumulative[:, :, None] - cumulative[:, None, :], 0.0)
    mask = jnp.where(lower[None], jnp.exp(gaps), 0.0)
    scores = jnp.einsum('hid,hjd->hij', queries.astype(jnp.float32), keys.astype(jnp.float32))
    block_weights = (scores * mask).astype(jnp.bfloat16)
    inner = jnp.einsum('hij,hjd->hid', block_weights.astype(jnp.float32), values.astype(jnp.float32))
    scaled = queries.astype(jnp.float32) * jnp.exp(cumulative)[:, :, None]
    carried = jnp.einsum('hid,hde->hie', scaled, state, precision=lax.Precision.HIGHEST)
    last = cumulative[:, -1]
    weighted_keys = keys.astype(jnp.float32) * jnp.exp(last[:, None] - cumulative)[:, :, None]
    update = jnp.einsum('hjd,hje->hde', weighted_keys, values.astype(jnp.float32), precision=lax.Precision.HIGHEST)
    new_state = jnp.exp(last)[:, None, None] * state + update
    return (new_state, inner + carried)

def reference(activations, w_qkv, w_out, log_decay):
    group = HEADS // N_TENSOR
    width = group * HEAD_DIM
    n_blocks = TOKENS // BLOCK
    total = jnp.zeros((TOKENS, D), jnp.float32)
    for index in range(N_TENSOR):
        weights = w_qkv[:, :, index * width:(index + 1) * width].reshape(D, 3 * width)
        projected = jnp.dot(activations, weights, preferred_element_type=jnp.float32)
        queries = jax.nn.silu(projected[:, :width]).astype(jnp.bfloat16)
        keys = jax.nn.silu(projected[:, width:2 * width]).astype(jnp.bfloat16)
        values = projected[:, 2 * width:].astype(jnp.bfloat16)

        def reshape_into_blocks(array):
            return array.reshape(n_blocks, BLOCK, group, HEAD_DIM).transpose(0, 2, 1, 3)
        decay = log_decay[index * group:(index + 1) * group].reshape(group, n_blocks, BLOCK).transpose(1, 0, 2)
        start = jnp.zeros((group, HEAD_DIM, HEAD_DIM), jnp.float32)
        _, attended_rows = lax.scan(block_step, start, (reshape_into_blocks(queries), reshape_into_blocks(keys), reshape_into_blocks(values), decay))
        normed = attended_rows * lax.rsqrt(lax.optimization_barrier(jnp.mean(attended_rows * attended_rows, axis=3, keepdims=True)) + 1e-06)
        flat = normed.transpose(0, 2, 1, 3).reshape(TOKENS, width).astype(jnp.bfloat16)
        partial_sum = jnp.dot(flat, w_out[index * width:(index + 1) * width], preferred_element_type=jnp.float32)
        total = total + partial_sum.astype(jnp.bfloat16).astype(jnp.float32)
    return total.astype(jnp.bfloat16)
```

```python
import functools

import jax
import jax.numpy as jnp
from jax import lax
from jax.experimental import pallas as pl
from jax.experimental.pallas import tpu as pltpu
from jax.sharding import PartitionSpec as P

HEAD_DIM = 128
BLOCK = 256
ROWS = 64
HEADS = 4
N_TENSOR = 8
N_Y = 4
IN_CHUNKS = 6
OUT_CHUNKS = 8
LAG = 2
AHEAD = 2
F32 = jnp.float32
BF16 = jnp.bfloat16


def silu(v):
    half = 0.5 * v
    return half + half * jnp.tanh(half)


def kernel(
    n_ctx, x_ref, w_ref, wo_ref, ld_ref, out_ref,
    xall, wv, w2, acc, q_s, qs_s, k_s, v_s, mask_s, eq_s, ek_s, inner_s, u_s,
    ld8, cum_s, elast_s, dsend, dec, edec,
    st1, rc1, st2, rc2, nsend, nrm, part, relay, summed, from_b, from_f,
    ag_send, ag_b, ag_f, ag_o, ag_s, own_sem, w_sem, wo_own, wo_send, wo_recv,
    dec_send, dec_recv, p1_send, p1_recv, p2_send, p2_recv, n_send, n_recv,
    rs_send, rs_relay, rs_b, rs_f, rs_sum_send,
):
    ctx = lax.axis_index("context")
    t = lax.axis_index("tensor")
    y = t // 2
    core = t % 2
    other = 1 - core
    sib = y * 2 + other
    d_model = x_ref.shape[1]
    kc = d_model // IN_CHUNKS
    nc = d_model // OUT_CHUNKS
    chunk_rows = HEADS * HEAD_DIM // n_ctx

    def remote(src, dst, send, recv, device):
        return pltpu.make_async_remote_copy(
            src_ref=src, dst_ref=dst, send_sem=send, recv_sem=recv,
            device_id=device, device_id_type=pl.DeviceIdType.MESH,
        )

    def ring(j):
        step = 1 - 2 * ((j + core) % 2)
        fwd = (y + step + N_Y) % N_Y
        bwd = (y - step + N_Y) % N_Y
        return fwd, bwd

    def in_cols(j):
        return pl.ds(pl.multiple_of(j * kc, kc), kc)

    def out_cols(j):
        return pl.ds(pl.multiple_of(j * nc, nc), nc)

    def w_copy(j):
        rows = in_cols(j)
        return pltpu.make_async_copy(w_ref.at[:, rows, :], wv.at[:, rows, :], w_sem.at[j])

    def own_copy(j):
        cols = in_cols(j)
        return pltpu.make_async_copy(x_ref.at[:, cols], xall.at[t, :, cols], own_sem.at[j])

    def send_own(j):
        cols = in_cols(j)
        fwd, bwd = ring(j)
        src, dst = x_ref.at[:, cols], xall.at[t, :, cols]
        remote(src, dst, ag_send, ag_b.at[j], {"tensor": fwd * 2 + core}).start()
        remote(src, dst, ag_send, ag_f.at[j], {"tensor": bwd * 2 + core}).start()
        remote(src, dst, ag_send, ag_s.at[j], {"tensor": sib}).start()

    def to_sibling(slot, j):
        part_ref = xall.at[slot, :, in_cols(j)]
        remote(part_ref, part_ref, ag_send, ag_s.at[j], {"tensor": sib}).start()

    def wait_slot(slot, j, sem):
        part_ref = xall.at[slot, :, in_cols(j)]
        remote(part_ref, part_ref, ag_send, sem.at[j], {"tensor": sib}).wait_recv()

    for j in range(IN_CHUNKS):
        own_copy(j).start()
        w_copy(j).start()
    wo_copy = pltpu.make_async_copy(wo_ref, w2.at[pl.ds(0, HEADS * HEAD_DIM)], wo_own)
    wo_copy.start()

    barrier = pltpu.get_barrier_semaphore()
    for peer in (((y + 1) % N_Y) * 2 + core, ((y + N_Y - 1) % N_Y) * 2 + core, sib):
        pl.semaphore_signal(
            barrier, inc=1, device_id={"tensor": peer}, device_id_type=pl.DeviceIdType.MESH
        )

    def greet(i, carry):
        pl.semaphore_signal(
            barrier, inc=1, device_id={"context": (ctx + i) % n_ctx},
            device_id_type=pl.DeviceIdType.MESH,
        )
        return carry

    lax.fori_loop(1, n_ctx, greet, 0)
    pl.semaphore_wait(barrier, 3 + n_ctx - 1)

    for j in range(AHEAD):
        send_own(j)

    ld8[0:HEADS, :] = ld_ref[:, 0:BLOCK]
    ld8[HEADS : 2 * HEADS, :] = ld_ref[:, BLOCK : 2 * BLOCK]
    cum = ld8[...]
    lane = lax.broadcasted_iota(jnp.int32, (2 * HEADS, BLOCK), 1)
    shift = 1
    while shift < BLOCK:
        cum = cum + jnp.where(lane >= shift, pltpu.roll(cum, shift, 1), 0.0)
        shift *= 2
    cum_s[...] = cum
    last = jnp.broadcast_to(cum[:, BLOCK - 1 : BLOCK], (2 * HEADS, HEAD_DIM))
    elast_s[...] = jnp.exp(last)
    both = last + pltpu.roll(last, HEADS, 0)
    dsend[...] = both
    dec[pl.ds(ctx, 1)] = both[None]

    def send_decay(i, carry):
        remote(
            dsend, dec.at[ctx], dec_send, dec_recv, {"context": (ctx + i) % n_ctx}
        ).start()
        return carry

    lax.fori_loop(1, n_ctx, send_decay, 0)

    def decay_tables(r, carry):
        row = cum_s[pl.ds(r, 1), :]
        column = jnp.transpose(jnp.broadcast_to(row, (HEAD_DIM, BLOCK)))
        end = row[:, BLOCK - 1 : BLOCK]
        eq_s[r] = jnp.exp(column).reshape(2, 2, ROWS, HEAD_DIM)
        ek_s[r] = jnp.exp(end - column)
        for half in range(2):
            at = half * HEAD_DIM
            gaps = jnp.minimum(column - row[:, at : at + HEAD_DIM], 0.0)
            i = lax.broadcasted_iota(jnp.int32, (BLOCK, HEAD_DIM), 0)
            k = lax.broadcasted_iota(jnp.int32, (BLOCK, HEAD_DIM), 1) + at
            mask_s[r, :, at : at + HEAD_DIM] = jnp.where(i >= k, jnp.exp(gaps), 0.0)
        return carry

    lax.fori_loop(0, 2 * HEADS, decay_tables, 0)
    acc[...] = jnp.zeros_like(acc)

    def forward(j):
        fwd, bwd = ring(j)
        wait_slot(bwd * 2 + core, j, ag_b)
        src = xall.at[bwd * 2 + core, :, in_cols(j)]
        remote(src, src, ag_send, ag_o.at[j], {"tensor": fwd * 2 + core}).start()
        to_sibling(bwd * 2 + core, j)
        wait_slot(fwd * 2 + core, j, ag_f)
        to_sibling(fwd * 2 + core, j)

    def opposite(j):
        slot = ((y + 2) % N_Y) * 2 + core
        wait_slot(slot, j, ag_o)
        to_sibling(slot, j)

    def finish(j):
        four = xall.at[pl.ds(0, 4), :, in_cols(j)]
        remote(four, four, ag_send, ag_s.at[j], {"tensor": sib}).wait_recv()
        own_copy(j).wait()
        w_copy(j).wait()

    def multiply(j, parts):
        rows = xall[:, :, in_cols(j)].reshape(N_TENSOR * ROWS, kc)
        for i in parts:
            acc[i] += jnp.dot(rows, wv[i, in_cols(j), :], preferred_element_type=F32)

    wo_rows = HEADS * HEAD_DIM // IN_CHUNKS // 16 * 16

    def send_w_out():
        remote(
            wo_ref, w2.at[pl.ds(HEADS * HEAD_DIM, HEADS * HEAD_DIM)],
            wo_send, wo_recv, {"tensor": sib},
        ).start()

    forward(0)

    def gather_step(j, carry):
        @pl.when(j + AHEAD - 1 < IN_CHUNKS)
        def _():
            send_own(j + AHEAD - 1)

        forward(j)
        opposite(j - 1)
        finish(j - 1)
        multiply(j - 1, (0, 1, 2))
        return carry

    send_w_out()
    lax.fori_loop(1, IN_CHUNKS, gather_step, 0)

    def decay_size():
        return remote(
            dec.at[pl.ds(0, n_ctx - 1)], dec.at[pl.ds(0, n_ctx - 1)],
            dec_send, dec_recv, {"tensor": sib},
        )

    decay_size().wait_recv()
    my_head = ctx * chunk_rows // HEAD_DIM
    for i in range(n_ctx):
        edec[i : i + 1, :] = jnp.exp(dec[i, pl.ds(my_head, 1), :])

    opposite(IN_CHUNKS - 1)
    finish(IN_CHUNKS - 1)
    multiply(IN_CHUNKS - 1, (1, 2))

    for h in range(HEADS):
        lanes = slice(h * HEAD_DIM, (h + 1) * HEAD_DIM)
        keys = silu(acc[1, :, lanes]).astype(BF16)
        values = acc[2, :, lanes].astype(BF16)
        k_s[h] = keys
        v_s[h] = values
        states = []
        for n in range(2):
            rows = slice(n * BLOCK, (n + 1) * BLOCK)
            weighted = (keys[rows].astype(F32) * ek_s[n * HEADS + h]).astype(BF16)
            states.append(
                lax.dot_general(
                    weighted, values[rows], (((0,), (0,)), ((), ())), preferred_element_type=F32
                )
            )
        u_s[h] = states[0]
        total = elast_s[HEADS + h : HEADS + h + 1, :] * states[0] + states[1]
        pieces = HEAD_DIM // chunk_rows
        st1[h * pieces : (h + 1) * pieces] = total.astype(BF16).reshape(
            pieces, chunk_rows, HEAD_DIM
        )

    def send_state(i, carry):
        to = (ctx + i) % n_ctx
        remote(st1.at[to], rc1.at[ctx], p1_send, p1_recv, {"context": to}).start()
        return carry

    lax.fori_loop(1, n_ctx, send_state, 0)
    rc1[pl.ds(ctx, 1)] = st1[pl.ds(ctx, 1)]

    multiply(IN_CHUNKS - 1, (0,))

    def attend(n):
        for h in range(HEADS):
            lanes = slice(h * HEAD_DIM, (h + 1) * HEAD_DIM)
            rows = slice(n * BLOCK, (n + 1) * BLOCK)
            queries = silu(acc[0, rows, lanes]).astype(BF16)
            weights = lax.dot_general(
                queries, k_s[h, rows, :], (((1,), (1,)), ((), ())), preferred_element_type=F32
            )
            weights = (weights * mask_s[n * HEADS + h]).astype(BF16)
            inner_s[h, 2 * n : 2 * n + 2] = jnp.dot(
                weights, v_s[h, rows, :], preferred_element_type=F32
            ).reshape(2, 2, ROWS, HEAD_DIM)
            scaled = queries.astype(F32).reshape(2, 2, ROWS, HEAD_DIM) * eq_s[n * HEADS + h]
            qs_s[h, 2 * n : 2 * n + 2] = scaled.astype(BF16)

    attend(0)

    def state_size(buffer, send, recv):
        piece = buffer.at[pl.ds(0, n_ctx - 1)]
        return remote(piece, piece, send, recv, {"tensor": sib})

    state_size(rc1, p1_send, p1_recv).wait_recv()
    running = jnp.zeros((chunk_rows, HEAD_DIM), F32)
    for i in range(n_ctx):
        st2[i] = running.astype(BF16)

        @pl.when(ctx != i)
        def _():
            remote(st2.at[i], rc2.at[ctx], p2_send, p2_recv, {"context": i}).start()

        running = running * edec[i : i + 1, :] + rc1[i].astype(F32)
    rc2[pl.ds(ctx, 1)] = st2[pl.ds(ctx, 1)]

    attend(1)

    state_size(rc2, p2_send, p2_recv).wait_recv()

    pieces = HEAD_DIM // chunk_rows

    def normalize(which, target):
        for h in range(HEADS):
            lanes = slice(h * HEAD_DIM, (h + 1) * HEAD_DIM)
            entering = rc2[h * pieces : (h + 1) * pieces].reshape(HEAD_DIM, HEAD_DIM)
            later = elast_s[h : h + 1, :] * entering.astype(F32) + u_s[h]
            for n, state in enumerate((entering, later.astype(BF16))):
                queries = qs_s[h, 2 * n : 2 * n + 2, which].reshape(2 * ROWS, HEAD_DIM)
                attended = inner_s[h, 2 * n : 2 * n + 2, which].reshape(
                    2 * ROWS, HEAD_DIM
                ) + jnp.dot(queries, state, preferred_element_type=F32)
                size = jnp.mean(attended * attended, axis=1, keepdims=True)
                normed = (attended * lax.rsqrt(size + 1e-06)).astype(BF16)
                target[2 * n : 2 * n + 2, :, lanes] = normed.reshape(2, ROWS, HEAD_DIM)

    width = HEADS * HEAD_DIM
    normalize(other, nsend)
    norm_copy = remote(
        nsend, nrm.at[:, :, pl.ds(width, width)], n_send, n_recv, {"tensor": sib}
    )
    norm_copy.start()
    normalize(core, nrm)
    wo_copy.wait()
    w2_half = w2.at[pl.ds(width, width)]
    wo_wait = remote(w2_half, w2_half, wo_send, wo_recv, {"tensor": sib})
    wo_wait.wait_recv()
    norm_copy.wait_recv()

    def project(j):
        cols = out_cols(j)
        rows = nrm[...].reshape(N_Y * ROWS, 2 * width)
        chunk = jnp.dot(rows, w2[:, cols], preferred_element_type=F32).astype(BF16)
        part[:, :, cols] = chunk.reshape(N_Y, ROWS, nc)
        fwd, bwd = ring(j)
        remote(
            part.at[(y + 2) % N_Y, :, cols], relay.at[:, cols],
            rs_send, rs_relay.at[j], {"tensor": fwd * 2 + core},
        ).start()
        remote(
            part.at[bwd, :, cols], from_f.at[:, cols],
            rs_send, rs_f.at[j], {"tensor": bwd * 2 + core},
        ).start()

    def pass_on(j):
        cols = out_cols(j)
        fwd, _ = ring(j)
        remote(
            relay.at[:, cols], relay.at[:, cols], rs_send, rs_relay.at[j], {"tensor": sib}
        ).wait_recv()
        summed[:, cols] = (
            part[pl.ds(fwd, 1), :, cols].reshape(ROWS, nc).astype(F32)
            + relay[:, cols].astype(F32)
        ).astype(BF16)
        remote(
            summed.at[:, cols], from_b.at[:, cols],
            rs_sum_send, rs_b.at[j], {"tensor": fwd * 2 + core},
        ).start()

    def finish_rows(j):
        cols = out_cols(j)
        remote(
            from_f.at[:, cols], from_f.at[:, cols], rs_send, rs_f.at[j], {"tensor": sib}
        ).wait_recv()
        remote(
            from_b.at[:, cols], from_b.at[:, cols], rs_send, rs_b.at[j], {"tensor": sib}
        ).wait_recv()
        out_ref[:, cols] = (
            part[pl.ds(y, 1), :, cols].reshape(ROWS, nc).astype(F32)
            + from_f[:, cols].astype(F32)
            + from_b[:, cols].astype(F32)
        ).astype(out_ref.dtype)

    def project_step(j, carry):
        project(j)

        @pl.when(j >= LAG)
        def _():
            pass_on(j - LAG)

        return carry

    lax.fori_loop(0, OUT_CHUNKS, project_step, 0)

    def pass_step(j, carry):
        pass_on(j)
        finish_rows(j - (OUT_CHUNKS - LAG))
        return carry

    lax.fori_loop(OUT_CHUNKS - LAG, OUT_CHUNKS, pass_step, 0)

    seven = xall.at[pl.ds(0, 7)]
    remote(seven, seven, ag_send, ag_s.at[0], {"tensor": sib}).wait_send()
    wo_wait.wait_send()
    decay_size().wait_send()
    state_size(st1, p1_send, p1_recv).wait_send()
    state_size(st2, p2_send, p2_recv).wait_send()
    norm_copy.wait_send()

    def finish_step(j, carry):
        finish_rows(j)
        return carry

    lax.fori_loop(LAG, OUT_CHUNKS, finish_step, 0)
    two = part.at[pl.ds(0, 2)]
    remote(two, two, rs_send, rs_f.at[0], {"tensor": sib}).wait_send()
    remote(summed, summed, rs_sum_send, rs_b.at[0], {"tensor": sib}).wait_send()


def body(n_ctx, activations, w_qkv, w_out, log_decay):
    rows, d_model = activations.shape
    width = HEADS * HEAD_DIM
    chunk_rows = width // n_ctx
    any_space = pl.BlockSpec(memory_space=pl.ANY)
    vmem = pl.BlockSpec(memory_space=pltpu.VMEM)
    dma = pltpu.SemaphoreType.DMA
    shard = N_TENSOR * rows
    scratch = [
        pltpu.VMEM((N_TENSOR, rows, d_model), BF16),
        pltpu.VMEM((3, d_model, width), BF16),
        pltpu.VMEM((2 * width, d_model), BF16),
        pltpu.VMEM((3, shard, width), F32),
        pltpu.VMEM((HEADS, shard, HEAD_DIM), BF16),
        pltpu.VMEM((HEADS, N_Y, 2, rows, HEAD_DIM), BF16),
        pltpu.VMEM((HEADS, shard, HEAD_DIM), BF16),
        pltpu.VMEM((HEADS, shard, HEAD_DIM), BF16),
        pltpu.VMEM((2 * HEADS, BLOCK, BLOCK), F32),
        pltpu.VMEM((2 * HEADS, 2, 2, rows, HEAD_DIM), F32),
        pltpu.VMEM((2 * HEADS, BLOCK, HEAD_DIM), F32),
        pltpu.VMEM((HEADS, N_Y, 2, rows, HEAD_DIM), F32),
        pltpu.VMEM((HEADS, HEAD_DIM, HEAD_DIM), F32),
        pltpu.VMEM((2 * HEADS, BLOCK), F32),
        pltpu.VMEM((2 * HEADS, BLOCK), F32),
        pltpu.VMEM((2 * HEADS, HEAD_DIM), F32),
        pltpu.VMEM((2 * HEADS, HEAD_DIM), F32),
        pltpu.VMEM((n_ctx, 2 * HEADS, HEAD_DIM), F32),
        pltpu.VMEM((n_ctx, HEAD_DIM), F32),
        pltpu.VMEM((n_ctx, chunk_rows, HEAD_DIM), BF16),
        pltpu.VMEM((n_ctx, chunk_rows, HEAD_DIM), BF16),
        pltpu.VMEM((n_ctx, chunk_rows, HEAD_DIM), BF16),
        pltpu.VMEM((n_ctx, chunk_rows, HEAD_DIM), BF16),
        pltpu.VMEM((N_Y, rows, width), BF16),
        pltpu.VMEM((N_Y, rows, 2 * width), BF16),
        pltpu.VMEM((N_Y, rows, d_model), BF16),
        pltpu.VMEM((rows, d_model), BF16),
        pltpu.VMEM((rows, d_model), BF16),
        pltpu.VMEM((rows, d_model), BF16),
        pltpu.VMEM((rows, d_model), BF16),
        dma,
        dma((IN_CHUNKS,)),
        dma((IN_CHUNKS,)),
        dma((IN_CHUNKS,)),
        dma((IN_CHUNKS,)),
        dma((IN_CHUNKS,)),
        dma((IN_CHUNKS,)),
        dma,
        dma,
        dma,
        dma,
        dma,
        dma,
        dma,
        dma,
        dma,
        dma,
        dma,
        dma,
        dma((OUT_CHUNKS,)),
        dma((OUT_CHUNKS,)),
        dma((OUT_CHUNKS,)),
        dma,
    ]
    return pl.pallas_call(
        functools.partial(kernel, n_ctx),
        out_shape=jax.ShapeDtypeStruct((rows, d_model), BF16),
        in_specs=[any_space, any_space, any_space, vmem],
        out_specs=vmem,
        scratch_shapes=scratch,
        compiler_params=pltpu.CompilerParams(
            collective_id=0, has_side_effects=True, vmem_limit_bytes=52 * 1024 * 1024
        ),
    )(activations, w_qkv.transpose(1, 0, 2), w_out, log_decay)


def solution(mesh):
    in_specs = (
        P(("context", "tensor"), None),
        P(None, None, "tensor"),
        P("tensor", None),
        P("tensor", "context"),
    )
    out_specs = P(("context", "tensor"), None)
    return jax.shard_map(
        functools.partial(body, mesh.shape["context"]),
        mesh=mesh, in_specs=in_specs, out_specs=out_specs, check_vma=False,
    )
```

```python
import functools

import jax
import jax.numpy as jnp
from jax import lax
from jax.experimental import pallas as pl
from jax.experimental.pallas import tpu as pltpu
from jax.sharding import PartitionSpec as P

HEAD_DIM = 128
BLOCK = 256
ROWS = 64
HEADS = 4
N_TENSOR = 8
N_Y = 4
IN_CHUNKS = (512,) * 6
N_IN = len(IN_CHUNKS)
OUT_CHUNKS = 6
LAG = 3
AHEAD = 2
OPP_LAG = 2
MUL_LAG = 3
F32 = jnp.float32
BF16 = jnp.bfloat16


def silu(v):
    half = 0.5 * v
    return half + half * jnp.tanh(half)


def kernel(
    n_ctx, x_ref, w_ref, wo_ref, ld_ref, out_ref,
    xall, wv, w2, acc, q_s, qs_s, k_s, v_s, mask_s, eq_s, ek_s, inner_s, u_s,
    ld4, ld8, cum_s, elast_s, dsend, dec, edec,
    st1, rc1, st2, rc2, nsend, nrm, part, relay, summed, from_b, from_f,
    ag_send, ag_b, ag_f, ag_o, ag_s, own_sem, w_sem, wo_own, wo_send, wo_recv,
    dec_send, dec_recv, p1_send, p1_recv, p2_send, p2_recv, n_send, n_recv,
    rs_send, rs_relay, rs_b, rs_f, rs_sum_send, ld_sem,
):
    ctx = lax.axis_index("context")
    t = lax.axis_index("tensor")
    y = t // 2
    core = t % 2
    other = 1 - core
    sib = y * 2 + other
    d_model = x_ref.shape[1]
    nc = d_model // OUT_CHUNKS
    chunk_rows = HEADS * HEAD_DIM // n_ctx

    n_x = 4
    n_z = n_ctx // n_x

    def hops(dz, dx):
        return min(dz, n_z - dz) + min(dx, n_x - dx)

    others = sorted(
        ((dz, dx) for dz in range(n_z) for dx in range(n_x) if dz or dx),
        key=lambda d: -hops(*d),
    )
    peers = [
        (ctx // n_x + dz) % n_z * n_x + (ctx % n_x + dx) % n_x for dz, dx in others
    ]

    def remote(src, dst, send, recv, device):
        return pltpu.make_async_remote_copy(
            src_ref=src, dst_ref=dst, send_sem=send, recv_sem=recv,
            device_id=device, device_id_type=pl.DeviceIdType.MESH,
        )

    def ring(j):
        step = 1 - 2 * ((j + core) % 2)
        fwd = (y + step + N_Y) % N_Y
        bwd = (y - step + N_Y) % N_Y
        return fwd, bwd

    def in_cols(j):
        return pl.ds(sum(IN_CHUNKS[:j]), IN_CHUNKS[j])

    def out_cols(j):
        return pl.ds(pl.multiple_of(j * nc, nc), nc)

    def w_copy(j):
        rows = in_cols(j)
        return pltpu.make_async_copy(w_ref.at[:, rows, :], wv.at[:, rows, :], w_sem.at[j])

    def own_copy(j):
        cols = in_cols(j)
        return pltpu.make_async_copy(x_ref.at[:, cols], xall.at[t, :, cols], own_sem.at[j])

    def send_own(j):
        cols = in_cols(j)
        fwd, bwd = ring(j)
        src, dst = x_ref.at[:, cols], xall.at[t, :, cols]
        remote(src, dst, ag_send, ag_b.at[j], {"tensor": fwd * 2 + core}).start()
        remote(src, dst, ag_send, ag_f.at[j], {"tensor": bwd * 2 + core}).start()
        remote(src, dst, ag_send, ag_s.at[j], {"tensor": sib}).start()

    def to_sibling(slot, j):
        part_ref = xall.at[slot, :, in_cols(j)]
        remote(part_ref, part_ref, ag_send, ag_s.at[j], {"tensor": sib}).start()

    def wait_slot(slot, j, sem):
        part_ref = xall.at[slot, :, in_cols(j)]
        remote(part_ref, part_ref, ag_send, sem.at[j], {"tensor": sib}).wait_recv()

    ld_copy = pltpu.make_async_copy(ld_ref, ld4, ld_sem)
    ld_copy.start()
    for j in range(N_IN):
        own_copy(j).start()
        w_copy(j).start()
    wo_copy = pltpu.make_async_copy(wo_ref, w2.at[pl.ds(0, HEADS * HEAD_DIM)], wo_own)
    wo_copy.start()

    barrier = pltpu.get_barrier_semaphore()
    for peer in (((y + 1) % N_Y) * 2 + core, ((y + N_Y - 1) % N_Y) * 2 + core, sib):
        pl.semaphore_signal(
            barrier, inc=1, device_id={"tensor": peer}, device_id_type=pl.DeviceIdType.MESH
        )

    def greet(i, carry):
        pl.semaphore_signal(
            barrier, inc=1, device_id={"context": (ctx + i) % n_ctx},
            device_id_type=pl.DeviceIdType.MESH,
        )
        return carry

    lax.fori_loop(1, n_ctx, greet, 0)
    pl.semaphore_wait(barrier, 3 + n_ctx - 1)

    for j in range(AHEAD):
        send_own(j)

    ld_copy.wait()
    ld8[0:HEADS, :] = ld4[:, 0:BLOCK]
    ld8[HEADS : 2 * HEADS, :] = ld4[:, BLOCK : 2 * BLOCK]
    cum = ld8[...]
    lane = lax.broadcasted_iota(jnp.int32, (2 * HEADS, BLOCK), 1)
    shift = 1
    while shift < BLOCK:
        cum = cum + jnp.where(lane >= shift, pltpu.roll(cum, shift, 1), 0.0)
        shift *= 2
    cum_s[...] = cum
    last = jnp.broadcast_to(cum[:, BLOCK - 1 : BLOCK], (2 * HEADS, HEAD_DIM))
    elast_s[...] = jnp.exp(last)
    both = last + pltpu.roll(last, HEADS, 0)
    dsend[...] = both
    dec[pl.ds(ctx, 1)] = both[None]

    def send_decay(i, carry):
        remote(
            dsend, dec.at[ctx], dec_send, dec_recv, {"context": (ctx + i) % n_ctx}
        ).start()
        return carry

    lax.fori_loop(1, n_ctx, send_decay, 0)

    def decay_tables(r):
        row = cum_s[pl.ds(r, 1), :]
        column = jnp.transpose(jnp.broadcast_to(row, (HEAD_DIM, BLOCK)))
        end = row[:, BLOCK - 1 : BLOCK]
        eq_s[r] = jnp.exp(column).reshape(2, 2, ROWS, HEAD_DIM)
        ek_s[r] = jnp.exp(end - column)
        for half in range(2):
            at = half * HEAD_DIM
            gaps = jnp.minimum(column - row[:, at : at + HEAD_DIM], 0.0)
            i = lax.broadcasted_iota(jnp.int32, (BLOCK, HEAD_DIM), 0)
            k = lax.broadcasted_iota(jnp.int32, (BLOCK, HEAD_DIM), 1) + at
            mask_s[r, :, at : at + HEAD_DIM] = jnp.where(i >= k, jnp.exp(gaps), 0.0)

    acc[...] = jnp.zeros_like(acc)

    def forward(j):
        fwd, bwd = ring(j)
        wait_slot(bwd * 2 + core, j, ag_b)
        src = xall.at[bwd * 2 + core, :, in_cols(j)]
        remote(src, src, ag_send, ag_o.at[j], {"tensor": fwd * 2 + core}).start()
        to_sibling(bwd * 2 + core, j)
        wait_slot(fwd * 2 + core, j, ag_f)
        to_sibling(fwd * 2 + core, j)

    def opposite(j):
        slot = ((y + 2) % N_Y) * 2 + core
        wait_slot(slot, j, ag_o)
        to_sibling(slot, j)

    def finish(j):
        four = xall.at[pl.ds(0, 4), :, in_cols(j)]
        remote(four, four, ag_send, ag_s.at[j], {"tensor": sib}).wait_recv()
        own_copy(j).wait()
        w_copy(j).wait()

    def multiply(j, parts):
        rows = xall[:, :, in_cols(j)].reshape(N_TENSOR * ROWS, IN_CHUNKS[j])
        for i in parts:
            acc[i] += jnp.dot(rows, wv[i, in_cols(j), :], preferred_element_type=F32)

    for j in range(N_IN + MUL_LAG - 1):
        if AHEAD <= j + AHEAD < N_IN:
            send_own(j + AHEAD)
        if j < N_IN:
            forward(j)
        if j < 2 * HEADS:
            decay_tables(j)
        if 0 <= j - OPP_LAG < N_IN:
            opposite(j - OPP_LAG)
        if 0 <= j - MUL_LAG < N_IN - 1:
            finish(j - MUL_LAG)
            multiply(j - MUL_LAG, (0, 1, 2))

    def decay_size():
        return remote(
            dec.at[pl.ds(0, n_ctx - 1)], dec.at[pl.ds(0, n_ctx - 1)],
            dec_send, dec_recv, {"tensor": sib},
        )

    decay_size().wait_recv()
    my_head = ctx * chunk_rows // HEAD_DIM
    for i in range(n_ctx):
        edec[i : i + 1, :] = jnp.exp(dec[i, pl.ds(my_head, 1), :])

    finish(N_IN - 1)
    multiply(N_IN - 1, (1, 2))
    remote(
        wo_ref, w2.at[pl.ds(HEADS * HEAD_DIM, HEADS * HEAD_DIM)],
        wo_send, wo_recv, {"tensor": sib},
    ).start()

    for h in range(HEADS):
        lanes = slice(h * HEAD_DIM, (h + 1) * HEAD_DIM)
        keys = silu(acc[1, :, lanes]).astype(BF16)
        values = acc[2, :, lanes].astype(BF16)
        k_s[h] = keys
        v_s[h] = values
        states = []
        for n in range(2):
            rows = slice(n * BLOCK, (n + 1) * BLOCK)
            weighted = (keys[rows].astype(F32) * ek_s[n * HEADS + h]).astype(BF16)
            states.append(
                lax.dot_general(
                    weighted, values[rows], (((0,), (0,)), ((), ())), preferred_element_type=F32
                )
            )
        u_s[h] = states[0]
        total = elast_s[HEADS + h : HEADS + h + 1, :] * states[0] + states[1]
        pieces = HEAD_DIM // chunk_rows
        st1[h * pieces : (h + 1) * pieces] = total.astype(BF16).reshape(
            pieces, chunk_rows, HEAD_DIM
        )

    for to in peers:
        remote(st1.at[to], rc1.at[ctx], p1_send, p1_recv, {"context": to}).start()
    rc1[pl.ds(ctx, 1)] = st1[pl.ds(ctx, 1)]

    multiply(N_IN - 1, (0,))

    def attend(n):
        for h in range(HEADS):
            lanes = slice(h * HEAD_DIM, (h + 1) * HEAD_DIM)
            rows = slice(n * BLOCK, (n + 1) * BLOCK)
            queries = silu(acc[0, rows, lanes]).astype(BF16)
            weights = lax.dot_general(
                queries, k_s[h, rows, :], (((1,), (1,)), ((), ())), preferred_element_type=F32
            )
            weights = (weights * mask_s[n * HEADS + h]).astype(BF16)
            inner_s[h, 2 * n : 2 * n + 2] = jnp.dot(
                weights, v_s[h, rows, :], preferred_element_type=F32
            ).reshape(2, 2, ROWS, HEAD_DIM)
            scaled = queries.astype(F32).reshape(2, 2, ROWS, HEAD_DIM) * eq_s[n * HEADS + h]
            qs_s[h, 2 * n : 2 * n + 2] = scaled.astype(BF16)

    attend(0)

    def state_size(buffer, send, recv):
        piece = buffer.at[pl.ds(0, n_ctx - 1)]
        return remote(piece, piece, send, recv, {"tensor": sib})

    state_size(rc1, p1_send, p1_recv).wait_recv()
    running = jnp.zeros((chunk_rows, HEAD_DIM), F32)
    for i in range(n_ctx):
        st2[i] = running.astype(BF16)
        running = running * edec[i : i + 1, :] + rc1[i].astype(F32)
    for to in peers:
        remote(st2.at[to], rc2.at[ctx], p2_send, p2_recv, {"context": to}).start()
    rc2[pl.ds(ctx, 1)] = st2[pl.ds(ctx, 1)]

    attend(1)

    state_size(rc2, p2_send, p2_recv).wait_recv()

    pieces = HEAD_DIM // chunk_rows

    def normalize(which, target):
        for h in range(HEADS):
            lanes = slice(h * HEAD_DIM, (h + 1) * HEAD_DIM)
            entering = rc2[h * pieces : (h + 1) * pieces].reshape(HEAD_DIM, HEAD_DIM)
            later = elast_s[h : h + 1, :] * entering.astype(F32) + u_s[h]
            for n, state in enumerate((entering, later.astype(BF16))):
                queries = qs_s[h, 2 * n : 2 * n + 2, which].reshape(2 * ROWS, HEAD_DIM)
                attended = inner_s[h, 2 * n : 2 * n + 2, which].reshape(
                    2 * ROWS, HEAD_DIM
                ) + jnp.dot(queries, state, preferred_element_type=F32)
                size = jnp.mean(attended * attended, axis=1, keepdims=True)
                normed = (attended * lax.rsqrt(size + 1e-06)).astype(BF16)
                target[2 * n : 2 * n + 2, :, lanes] = normed.reshape(2, ROWS, HEAD_DIM)

    width = HEADS * HEAD_DIM
    normalize(other, nsend)
    norm_copy = remote(
        nsend, nrm.at[:, :, pl.ds(width, width)], n_send, n_recv, {"tensor": sib}
    )
    norm_copy.start()
    normalize(core, nrm)
    wo_copy.wait()
    w2_half = w2.at[pl.ds(width, width)]
    wo_wait = remote(w2_half, w2_half, wo_send, wo_recv, {"tensor": sib})
    wo_wait.wait_recv()
    norm_copy.wait_recv()

    def project(j):
        cols = out_cols(j)
        rows = nrm[...].reshape(N_Y * ROWS, 2 * width)
        chunk = jnp.dot(rows, w2[:, cols], preferred_element_type=F32).astype(BF16)
        part[:, :, cols] = chunk.reshape(N_Y, ROWS, nc)
        fwd, bwd = ring(j)
        remote(
            part.at[(y + 2) % N_Y, :, cols], relay.at[:, cols],
            rs_send, rs_relay.at[j], {"tensor": fwd * 2 + core},
        ).start()
        remote(
            part.at[bwd, :, cols], from_f.at[:, cols],
            rs_send, rs_f.at[j], {"tensor": bwd * 2 + core},
        ).start()

    def pass_on(j):
        cols = out_cols(j)
        fwd, _ = ring(j)
        remote(
            relay.at[:, cols], relay.at[:, cols], rs_send, rs_relay.at[j], {"tensor": sib}
        ).wait_recv()
        summed[:, cols] = (
            part[pl.ds(fwd, 1), :, cols].reshape(ROWS, nc).astype(F32)
            + relay[:, cols].astype(F32)
        ).astype(BF16)
        remote(
            summed.at[:, cols], from_b.at[:, cols],
            rs_sum_send, rs_b.at[j], {"tensor": fwd * 2 + core},
        ).start()

    def finish_rows(j):
        cols = out_cols(j)
        remote(
            from_f.at[:, cols], from_f.at[:, cols], rs_send, rs_f.at[j], {"tensor": sib}
        ).wait_recv()
        remote(
            from_b.at[:, cols], from_b.at[:, cols], rs_send, rs_b.at[j], {"tensor": sib}
        ).wait_recv()
        out_ref[:, cols] = (
            part[pl.ds(y, 1), :, cols].reshape(ROWS, nc).astype(F32)
            + from_f[:, cols].astype(F32)
            + from_b[:, cols].astype(F32)
        ).astype(out_ref.dtype)

    def project_step(j, carry):
        project(j)

        @pl.when(j >= LAG)
        def _():
            pass_on(j - LAG)

        return carry

    lax.fori_loop(0, OUT_CHUNKS, project_step, 0)

    def pass_step(j, carry):
        pass_on(j)
        finish_rows(j - (OUT_CHUNKS - LAG))
        return carry

    lax.fori_loop(OUT_CHUNKS - LAG, OUT_CHUNKS, pass_step, 0)

    seven = xall.at[pl.ds(0, 7)]
    remote(seven, seven, ag_send, ag_s.at[0], {"tensor": sib}).wait_send()
    wo_wait.wait_send()
    decay_size().wait_send()
    state_size(st1, p1_send, p1_recv).wait_send()
    state_size(st2, p2_send, p2_recv).wait_send()
    norm_copy.wait_send()

    def finish_step(j, carry):
        finish_rows(j)
        return carry

    lax.fori_loop(LAG, OUT_CHUNKS, finish_step, 0)
    two = part.at[pl.ds(0, 2)]
    remote(two, two, rs_send, rs_f.at[0], {"tensor": sib}).wait_send()
    remote(summed, summed, rs_sum_send, rs_b.at[0], {"tensor": sib}).wait_send()


def body(n_ctx, activations, w_qkv, w_out, log_decay):
    rows, d_model = activations.shape
    width = HEADS * HEAD_DIM
    chunk_rows = width // n_ctx
    hbm = pl.BlockSpec(memory_space=pltpu.HBM)
    vmem = pl.BlockSpec(memory_space=pltpu.VMEM)
    dma = pltpu.SemaphoreType.DMA
    shard = N_TENSOR * rows
    scratch = [
        pltpu.VMEM((N_TENSOR, rows, d_model), BF16),
        pltpu.VMEM((3, d_model, width), BF16),
        pltpu.VMEM((2 * width, d_model), BF16),
        pltpu.VMEM((3, shard, width), F32),
        pltpu.VMEM((HEADS, shard, HEAD_DIM), BF16),
        pltpu.VMEM((HEADS, N_Y, 2, rows, HEAD_DIM), BF16),
        pltpu.VMEM((HEADS, shard, HEAD_DIM), BF16),
        pltpu.VMEM((HEADS, shard, HEAD_DIM), BF16),
        pltpu.VMEM((2 * HEADS, BLOCK, BLOCK), F32),
        pltpu.VMEM((2 * HEADS, 2, 2, rows, HEAD_DIM), F32),
        pltpu.VMEM((2 * HEADS, BLOCK, HEAD_DIM), F32),
        pltpu.VMEM((HEADS, N_Y, 2, rows, HEAD_DIM), F32),
        pltpu.VMEM((HEADS, HEAD_DIM, HEAD_DIM), F32),
        pltpu.VMEM((HEADS, 2 * BLOCK), F32),
        pltpu.VMEM((2 * HEADS, BLOCK), F32),
        pltpu.VMEM((2 * HEADS, BLOCK), F32),
        pltpu.VMEM((2 * HEADS, HEAD_DIM), F32),
        pltpu.VMEM((2 * HEADS, HEAD_DIM), F32),
        pltpu.VMEM((n_ctx, 2 * HEADS, HEAD_DIM), F32),
        pltpu.VMEM((n_ctx, HEAD_DIM), F32),
        pltpu.VMEM((n_ctx, chunk_rows, HEAD_DIM), BF16),
        pltpu.VMEM((n_ctx, chunk_rows, HEAD_DIM), BF16),
        pltpu.VMEM((n_ctx, chunk_rows, HEAD_DIM), BF16),
        pltpu.VMEM((n_ctx, chunk_rows, HEAD_DIM), BF16),
        pltpu.VMEM((N_Y, rows, width), BF16),
        pltpu.VMEM((N_Y, rows, 2 * width), BF16),
        pltpu.VMEM((N_Y, rows, d_model), BF16),
        pltpu.VMEM((rows, d_model), BF16),
        pltpu.VMEM((rows, d_model), BF16),
        pltpu.VMEM((rows, d_model), BF16),
        pltpu.VMEM((rows, d_model), BF16),
        dma,
        dma((N_IN,)),
        dma((N_IN,)),
        dma((N_IN,)),
        dma((N_IN,)),
        dma((N_IN,)),
        dma((N_IN,)),
        dma,
        dma,
        dma,
        dma,
        dma,
        dma,
        dma,
        dma,
        dma,
        dma,
        dma,
        dma,
        dma((OUT_CHUNKS,)),
        dma((OUT_CHUNKS,)),
        dma((OUT_CHUNKS,)),
        dma,
        dma,
    ]
    return pl.pallas_call(
        functools.partial(kernel, n_ctx),
        out_shape=jax.ShapeDtypeStruct((rows, d_model), BF16),
        in_specs=[hbm, hbm, hbm, hbm],
        out_specs=vmem,
        scratch_shapes=scratch,
        compiler_params=pltpu.CompilerParams(
            collective_id=0, has_side_effects=True, vmem_limit_bytes=52 * 1024 * 1024
        ),
    )(*(
        pltpu.with_memory_space_constraint(array, pltpu.HBM)
        for array in (activations, w_qkv.transpose(1, 0, 2), w_out, log_decay)
    ))


def solution(mesh):
    in_specs = (
        P(("context", "tensor"), None),
        P(None, None, "tensor"),
        P("tensor", None),
        P("tensor", "context"),
    )
    out_specs = P(("context", "tensor"), None)
    return jax.shard_map(
        functools.partial(body, mesh.shape["context"]),
        mesh=mesh, in_specs=in_specs, out_specs=out_specs, check_vma=False,
    )
```

```python
import functools

import jax
import jax.numpy as jnp
from jax import lax
from jax.experimental import pallas as pl
from jax.experimental.pallas import tpu as pltpu
from jax.sharding import PartitionSpec as P

HEAD_DIM = 128
BLOCK = 256
ROWS = 64
HEADS = 4
N_TENSOR = 8
N_Y = 4
IN_CHUNKS = (512,) * 6
N_IN = len(IN_CHUNKS)
OUT_CHUNKS = 6
LAG = 3
EARLY = 2
OWN, UP, DOWN, OPPOSITE = range(N_Y)
F32 = jnp.float32
BF16 = jnp.bfloat16


def silu(v):
    half = 0.5 * v
    return half + half * jnp.tanh(half)


def kernel(
    n_ctx, x_ref, w_ref, wo_ref, ld_ref, out_ref,
    xall, wv, w2, acc, qs_s, k_s, v_s, mask_s, eq_s, ek_s, inner_s, u_s,
    ld4, ld8, cum_s, elast_s, dsend, dec, edec,
    st1, rc1, st2, rc2, nsend, nrm, part, relay, summed, from_b, from_f,
    ag_send, ag_up, ag_down, ag_o, ag_s, ag_so, own_sem, w_sem, wo_own, wo_send, wo_recv,
    dec_send, dec_recv, p1_send, p1_recv, p2_send, p2_recv, n_send, n_recv,
    rs_send, rs_relay, rs_b, rs_f, rs_sum_send, ld_sem,
):
    ctx = lax.axis_index("context")
    t = lax.axis_index("tensor")
    y = t // 2
    core = t % 2
    other = 1 - core
    sib = y * 2 + other
    d_model = x_ref.shape[1]
    nc = d_model // OUT_CHUNKS
    chunk_rows = HEADS * HEAD_DIM // n_ctx

    n_x = 4
    n_z = n_ctx // n_x

    def hops(dz, dx):
        return min(dz, n_z - dz) + min(dx, n_x - dx)

    others = sorted(
        ((dz, dx) for dz in range(n_z) for dx in range(n_x) if dz or dx),
        key=lambda d: -hops(*d),
    )
    peers = [
        (ctx // n_x + dz) % n_z * n_x + (ctx % n_x + dx) % n_x for dz, dx in others
    ]

    def remote(src, dst, send, recv, device):
        return pltpu.make_async_remote_copy(
            src_ref=src, dst_ref=dst, send_sem=send, recv_sem=recv,
            device_id=device, device_id_type=pl.DeviceIdType.MESH,
        )

    def ring(j):
        step = 1 - 2 * ((j + core) % 2)
        fwd = (y + step + N_Y) % N_Y
        bwd = (y - step + N_Y) % N_Y
        return fwd, bwd

    def in_cols(j):
        return pl.ds(sum(IN_CHUNKS[:j]), IN_CHUNKS[j])

    def out_cols(j):
        return pl.ds(pl.multiple_of(j * nc, nc), nc)

    def w_copy(j):
        rows = in_cols(j)
        return pltpu.make_async_copy(w_ref.at[:, rows, :], wv.at[:, rows, :], w_sem.at[j])

    def own_copy(j):
        cols = in_cols(j)
        return pltpu.make_async_copy(x_ref.at[:, cols], xall.at[OWN, core, :, cols], own_sem.at[j])

    up, down = (y + 1) % N_Y * 2, (y + N_Y - 1) % N_Y * 2

    def send_own(j):
        cols = in_cols(j)
        src = xall.at[OWN, core, :, cols]
        own_copy(j).wait()
        remote(
            src, xall.at[DOWN, core, :, cols], ag_send, ag_down.at[j], {"tensor": up + core}
        ).start()
        remote(
            src, xall.at[UP, core, :, cols], ag_send, ag_up.at[j], {"tensor": down + core}
        ).start()
        remote(src, src, ag_send, ag_s.at[j], {"tensor": sib}).start()

    def arrived(ref, sem):
        remote(ref, ref, ag_send, sem, {"tensor": sib}).wait_recv()

    def pass_near(j):
        cols = in_cols(j)
        arrived(xall.at[DOWN, core, :, cols], ag_down.at[j])
        arrived(xall.at[UP, core, :, cols], ag_up.at[j])
        upward = (j + core) % 2
        chip = (y + 2 * upward + N_Y - 1) % N_Y * 2
        src = xall.at[UP + upward, core, :, cols]
        dst = xall.at[OPPOSITE, core, :, cols]
        remote(src, dst, ag_send, ag_o.at[j], {"tensor": chip + core}).start()
        if j == N_IN - 1:
            remote(src, dst, ag_send, ag_so.at[j], {"tensor": chip + other}).start()
        near = xall.at[pl.ds(UP, 2), core, :, cols]
        remote(near, near, ag_send, ag_s.at[j], {"tensor": sib}).start()

    def pass_opposite(j):
        ref = xall.at[OPPOSITE, core, :, in_cols(j)]
        arrived(ref, ag_o.at[j])
        if j < N_IN - 1:
            remote(ref, ref, ag_send, ag_so.at[j], {"tensor": sib}).start()

    def multiply(j, slots, parts):
        first, count = slots
        rows = slice(first * 2 * ROWS, (first + count) * 2 * ROWS)
        values = xall[first : first + count, :, :, in_cols(j)].reshape(
            count * 2 * ROWS, IN_CHUNKS[j]
        )
        for i in parts:
            product = jnp.dot(values, wv[i, in_cols(j), :], preferred_element_type=F32)
            acc[i, rows] = product if j == 0 else acc[i, rows] + product

    def multiply_near(j):
        w_copy(j).wait()
        arrived(xall.at[pl.ds(OWN, 3), other, :, in_cols(j)], ag_s.at[j])
        multiply(j, (OWN, 3), (0, 1, 2))

    def multiply_opposite(j):
        arrived(xall.at[OPPOSITE, other, :, in_cols(j)], ag_so.at[j])
        multiply(j, (OPPOSITE, 1), (1, 2))

    def rows_of(i, chip, lanes):
        ahead = (chip - y + N_Y) % N_Y
        slot = ahead + ahead // 2 * (5 - 2 * ahead)
        return acc[i, pl.ds(pl.multiple_of(slot * 2 * ROWS, 2 * ROWS), 2 * ROWS), lanes]

    def block_of(i, n, lanes):
        return jnp.concatenate([rows_of(i, 2 * n, lanes), rows_of(i, 2 * n + 1, lanes)], axis=0)

    ld_copy = pltpu.make_async_copy(ld_ref, ld4, ld_sem)
    ld_copy.start()
    for j in range(N_IN):
        own_copy(j).start()
        w_copy(j).start()
    wo_copy = pltpu.make_async_copy(wo_ref, w2.at[pl.ds(0, HEADS * HEAD_DIM)], wo_own)
    wo_copy.start()

    barrier = pltpu.get_barrier_semaphore()
    for peer in (up + core, down + core, sib, up + other, down + other):
        pl.semaphore_signal(
            barrier, inc=1, device_id={"tensor": peer}, device_id_type=pl.DeviceIdType.MESH
        )

    def greet(i, carry):
        pl.semaphore_signal(
            barrier, inc=1, device_id={"context": (ctx + i) % n_ctx},
            device_id_type=pl.DeviceIdType.MESH,
        )
        return carry

    lax.fori_loop(1, n_ctx, greet, 0)
    pl.semaphore_wait(barrier, 5 + n_ctx - 1)

    for j in range(N_IN):
        send_own(j)

    ld_copy.wait()
    ld8[0:HEADS, :] = ld4[:, 0:BLOCK]
    ld8[HEADS : 2 * HEADS, :] = ld4[:, BLOCK : 2 * BLOCK]
    cum = ld8[...]
    lane = lax.broadcasted_iota(jnp.int32, (2 * HEADS, BLOCK), 1)
    shift = 1
    while shift < BLOCK:
        cum = cum + jnp.where(lane >= shift, pltpu.roll(cum, shift, 1), 0.0)
        shift *= 2
    cum_s[...] = cum
    last = jnp.broadcast_to(cum[:, BLOCK - 1 : BLOCK], (2 * HEADS, HEAD_DIM))
    elast_s[...] = jnp.exp(last)
    both = last + pltpu.roll(last, HEADS, 0)
    dsend[...] = both
    dec[pl.ds(ctx, 1)] = both[None]

    def send_decay(i, carry):
        remote(
            dsend, dec.at[ctx], dec_send, dec_recv, {"context": (ctx + i) % n_ctx}
        ).start()
        return carry

    lax.fori_loop(1, n_ctx, send_decay, 0)

    def decay_tables(r):
        row = cum_s[pl.ds(r, 1), :]
        column = jnp.transpose(jnp.broadcast_to(row, (HEAD_DIM, BLOCK)))
        end = row[:, BLOCK - 1 : BLOCK]
        eq_s[r] = jnp.exp(column).reshape(2, 2, ROWS, HEAD_DIM)
        ek_s[r] = jnp.exp(end - column)
        for half in range(2):
            at = half * HEAD_DIM
            gaps = jnp.minimum(column - row[:, at : at + HEAD_DIM], 0.0)
            i = lax.broadcasted_iota(jnp.int32, (BLOCK, HEAD_DIM), 0)
            k = lax.broadcasted_iota(jnp.int32, (BLOCK, HEAD_DIM), 1) + at
            mask_s[r, :, at : at + HEAD_DIM] = jnp.where(i >= k, jnp.exp(gaps), 0.0)

    for j in range(N_IN + 1):
        if j < N_IN:
            pass_near(j)
        for r in range(2 * HEADS):
            if r * (N_IN + 1) // (2 * HEADS) == j:
                decay_tables(r)
        if j == N_IN:
            for k in range(EARLY):
                pass_opposite(k)
        if j > 0:
            multiply_near(j - 1)

    def decay_size():
        return remote(
            dec.at[pl.ds(0, n_ctx - 1)], dec.at[pl.ds(0, n_ctx - 1)],
            dec_send, dec_recv, {"tensor": sib},
        )

    decay_size().wait_recv()
    my_head = ctx * chunk_rows // HEAD_DIM
    for i in range(n_ctx):
        edec[i : i + 1, :] = jnp.exp(dec[i, pl.ds(my_head, 1), :])

    for j in range(EARLY, N_IN + EARLY):
        if j < N_IN:
            pass_opposite(j)
        multiply_opposite(j - EARLY)
    remote(
        wo_ref, w2.at[pl.ds(HEADS * HEAD_DIM, HEADS * HEAD_DIM)],
        wo_send, wo_recv, {"tensor": sib},
    ).start()

    for h in range(HEADS):
        lanes = slice(h * HEAD_DIM, (h + 1) * HEAD_DIM)
        states = []
        for n in range(2):
            rows = slice(n * BLOCK, (n + 1) * BLOCK)
            keys = silu(block_of(1, n, lanes)).astype(BF16)
            values = block_of(2, n, lanes).astype(BF16)
            k_s[h, rows] = keys
            v_s[h, rows] = values
            weighted = (keys.astype(F32) * ek_s[n * HEADS + h]).astype(BF16)
            states.append(
                lax.dot_general(
                    weighted, values, (((0,), (0,)), ((), ())), preferred_element_type=F32
                )
            )
        u_s[h] = states[0]
        total = elast_s[HEADS + h : HEADS + h + 1, :] * states[0] + states[1]
        pieces = HEAD_DIM // chunk_rows
        st1[h * pieces : (h + 1) * pieces] = total.astype(BF16).reshape(
            pieces, chunk_rows, HEAD_DIM
        )

    for to in peers:
        remote(st1.at[to], rc1.at[ctx], p1_send, p1_recv, {"context": to}).start()
    rc1[pl.ds(ctx, 1)] = st1[pl.ds(ctx, 1)]

    for j in range(N_IN):
        multiply(j, (OPPOSITE, 1), (0,))

    def attend(n):
        for h in range(HEADS):
            lanes = slice(h * HEAD_DIM, (h + 1) * HEAD_DIM)
            rows = slice(n * BLOCK, (n + 1) * BLOCK)
            queries = silu(block_of(0, n, lanes)).astype(BF16)
            weights = lax.dot_general(
                queries, k_s[h, rows, :], (((1,), (1,)), ((), ())), preferred_element_type=F32
            )
            weights = (weights * mask_s[n * HEADS + h]).astype(BF16)
            inner_s[h, 2 * n : 2 * n + 2] = jnp.dot(
                weights, v_s[h, rows, :], preferred_element_type=F32
            ).reshape(2, 2, ROWS, HEAD_DIM)
            scaled = queries.astype(F32).reshape(2, 2, ROWS, HEAD_DIM) * eq_s[n * HEADS + h]
            qs_s[h, 2 * n : 2 * n + 2] = scaled.astype(BF16)

    attend(0)

    def state_size(buffer, send, recv):
        piece = buffer.at[pl.ds(0, n_ctx - 1)]
        return remote(piece, piece, send, recv, {"tensor": sib})

    state_size(rc1, p1_send, p1_recv).wait_recv()
    running = jnp.zeros((chunk_rows, HEAD_DIM), F32)
    for i in range(n_ctx):
        st2[i] = running.astype(BF16)
        running = running * edec[i : i + 1, :] + rc1[i].astype(F32)
    for to in peers:
        remote(st2.at[to], rc2.at[ctx], p2_send, p2_recv, {"context": to}).start()
    rc2[pl.ds(ctx, 1)] = st2[pl.ds(ctx, 1)]

    attend(1)

    state_size(rc2, p2_send, p2_recv).wait_recv()

    pieces = HEAD_DIM // chunk_rows

    def normalize(which, target):
        for h in range(HEADS):
            lanes = slice(h * HEAD_DIM, (h + 1) * HEAD_DIM)
            entering = rc2[h * pieces : (h + 1) * pieces].reshape(HEAD_DIM, HEAD_DIM)
            later = elast_s[h : h + 1, :] * entering.astype(F32) + u_s[h]
            for n, state in enumerate((entering, later.astype(BF16))):
                queries = qs_s[h, 2 * n : 2 * n + 2, which].reshape(2 * ROWS, HEAD_DIM)
                attended = inner_s[h, 2 * n : 2 * n + 2, which].reshape(
                    2 * ROWS, HEAD_DIM
                ) + jnp.dot(queries, state, preferred_element_type=F32)
                size = jnp.mean(attended * attended, axis=1, keepdims=True)
                normed = (attended * lax.rsqrt(size + 1e-06)).astype(BF16)
                target[2 * n : 2 * n + 2, :, lanes] = normed.reshape(2, ROWS, HEAD_DIM)

    width = HEADS * HEAD_DIM
    normalize(other, nsend)
    norm_copy = remote(
        nsend, nrm.at[:, :, pl.ds(width, width)], n_send, n_recv, {"tensor": sib}
    )
    norm_copy.start()
    normalize(core, nrm)
    wo_copy.wait()
    w2_half = w2.at[pl.ds(width, width)]
    wo_wait = remote(w2_half, w2_half, wo_send, wo_recv, {"tensor": sib})
    wo_wait.wait_recv()
    norm_copy.wait_recv()

    def project(j):
        cols = out_cols(j)
        rows = nrm[...].reshape(N_Y * ROWS, 2 * width)
        chunk = jnp.dot(rows, w2[:, cols], preferred_element_type=F32).astype(BF16)
        part[:, :, cols] = chunk.reshape(N_Y, ROWS, nc)
        fwd, bwd = ring(j)
        remote(
            part.at[(y + 2) % N_Y, :, cols], relay.at[:, cols],
            rs_send, rs_relay.at[j], {"tensor": fwd * 2 + core},
        ).start()
        remote(
            part.at[bwd, :, cols], from_f.at[:, cols],
            rs_send, rs_f.at[j], {"tensor": bwd * 2 + core},
        ).start()

    def pass_on(j):
        cols = out_cols(j)
        fwd, _ = ring(j)
        remote(
            relay.at[:, cols], relay.at[:, cols], rs_send, rs_relay.at[j], {"tensor": sib}
        ).wait_recv()
        summed[:, cols] = (
            part[pl.ds(fwd, 1), :, cols].reshape(ROWS, nc).astype(F32)
            + relay[:, cols].astype(F32)
        ).astype(BF16)
        remote(
            summed.at[:, cols], from_b.at[:, cols],
            rs_sum_send, rs_b.at[j], {"tensor": fwd * 2 + core},
        ).start()

    def finish_rows(j):
        cols = out_cols(j)
        remote(
            from_f.at[:, cols], from_f.at[:, cols], rs_send, rs_f.at[j], {"tensor": sib}
        ).wait_recv()
        remote(
            from_b.at[:, cols], from_b.at[:, cols], rs_send, rs_b.at[j], {"tensor": sib}
        ).wait_recv()
        out_ref[:, cols] = (
            part[pl.ds(y, 1), :, cols].reshape(ROWS, nc).astype(F32)
            + from_f[:, cols].astype(F32)
            + from_b[:, cols].astype(F32)
        ).astype(out_ref.dtype)

    def project_step(j, carry):
        project(j)

        @pl.when(j >= LAG)
        def _():
            pass_on(j - LAG)

        return carry

    lax.fori_loop(0, OUT_CHUNKS, project_step, 0)

    def pass_step(j, carry):
        pass_on(j)
        finish_rows(j - (OUT_CHUNKS - LAG))
        return carry

    lax.fori_loop(OUT_CHUNKS - LAG, OUT_CHUNKS, pass_step, 0)

    seven = w2.at[pl.ds(0, 7 * ROWS)]
    remote(seven, seven, ag_send, ag_s.at[0], {"tensor": sib}).wait_send()
    wo_wait.wait_send()
    decay_size().wait_send()
    state_size(st1, p1_send, p1_recv).wait_send()
    state_size(st2, p2_send, p2_recv).wait_send()
    norm_copy.wait_send()

    def finish_step(j, carry):
        finish_rows(j)
        return carry

    lax.fori_loop(LAG, OUT_CHUNKS, finish_step, 0)
    two = part.at[pl.ds(0, 2)]
    remote(two, two, rs_send, rs_f.at[0], {"tensor": sib}).wait_send()
    remote(summed, summed, rs_sum_send, rs_b.at[0], {"tensor": sib}).wait_send()


def body(n_ctx, activations, w_qkv, w_out, log_decay):
    rows, d_model = activations.shape
    width = HEADS * HEAD_DIM
    chunk_rows = width // n_ctx
    hbm = pl.BlockSpec(memory_space=pltpu.HBM)
    vmem = pl.BlockSpec(memory_space=pltpu.VMEM)
    dma = pltpu.SemaphoreType.DMA
    shard = N_TENSOR * rows
    scratch = [
        pltpu.VMEM((N_Y, 2, rows, d_model), BF16),
        pltpu.VMEM((3, d_model, width), BF16),
        pltpu.VMEM((2 * width, d_model), BF16),
        pltpu.VMEM((3, shard, width), F32),
        pltpu.VMEM((HEADS, N_Y, 2, rows, HEAD_DIM), BF16),
        pltpu.VMEM((HEADS, shard, HEAD_DIM), BF16),
        pltpu.VMEM((HEADS, shard, HEAD_DIM), BF16),
        pltpu.VMEM((2 * HEADS, BLOCK, BLOCK), F32),
        pltpu.VMEM((2 * HEADS, 2, 2, rows, HEAD_DIM), F32),
        pltpu.VMEM((2 * HEADS, BLOCK, HEAD_DIM), F32),
        pltpu.VMEM((HEADS, N_Y, 2, rows, HEAD_DIM), F32),
        pltpu.VMEM((HEADS, HEAD_DIM, HEAD_DIM), F32),
        pltpu.VMEM((HEADS, 2 * BLOCK), F32),
        pltpu.VMEM((2 * HEADS, BLOCK), F32),
        pltpu.VMEM((2 * HEADS, BLOCK), F32),
        pltpu.VMEM((2 * HEADS, HEAD_DIM), F32),
        pltpu.VMEM((2 * HEADS, HEAD_DIM), F32),
        pltpu.VMEM((n_ctx, 2 * HEADS, HEAD_DIM), F32),
        pltpu.VMEM((n_ctx, HEAD_DIM), F32),
        pltpu.VMEM((n_ctx, chunk_rows, HEAD_DIM), BF16),
        pltpu.VMEM((n_ctx, chunk_rows, HEAD_DIM), BF16),
        pltpu.VMEM((n_ctx, chunk_rows, HEAD_DIM), BF16),
        pltpu.VMEM((n_ctx, chunk_rows, HEAD_DIM), BF16),
        pltpu.VMEM((N_Y, rows, width), BF16),
        pltpu.VMEM((N_Y, rows, 2 * width), BF16),
        pltpu.VMEM((N_Y, rows, d_model), BF16),
        pltpu.VMEM((rows, d_model), BF16),
        pltpu.VMEM((rows, d_model), BF16),
        pltpu.VMEM((rows, d_model), BF16),
        pltpu.VMEM((rows, d_model), BF16),
        dma,
        dma((N_IN,)),
        dma((N_IN,)),
        dma((N_IN,)),
        dma((N_IN,)),
        dma((N_IN,)),
        dma((N_IN,)),
        dma((N_IN,)),
        dma,
        dma,
        dma,
        dma,
        dma,
        dma,
        dma,
        dma,
        dma,
        dma,
        dma,
        dma,
        dma((OUT_CHUNKS,)),
        dma((OUT_CHUNKS,)),
        dma((OUT_CHUNKS,)),
        dma,
        dma,
    ]
    return pl.pallas_call(
        functools.partial(kernel, n_ctx),
        out_shape=jax.ShapeDtypeStruct((rows, d_model), BF16),
        in_specs=[hbm, hbm, hbm, hbm],
        out_specs=vmem,
        scratch_shapes=scratch,
        compiler_params=pltpu.CompilerParams(
            collective_id=0, has_side_effects=True, vmem_limit_bytes=52 * 1024 * 1024
        ),
    )(*(
        pltpu.with_memory_space_constraint(array, pltpu.HBM)
        for array in (activations, w_qkv.transpose(1, 0, 2), w_out, log_decay)
    ))


def solution(mesh):
    in_specs = (
        P(("context", "tensor"), None),
        P(None, None, "tensor"),
        P("tensor", None),
        P("tensor", "context"),
    )
    out_specs = P(("context", "tensor"), None)
    return jax.shard_map(
        functools.partial(body, mesh.shape["context"]),
        mesh=mesh, in_specs=in_specs, out_specs=out_specs, check_vma=False,
    )
```

```python
import functools

import jax
import jax.numpy as jnp
from jax import lax
from jax.experimental import pallas as pl
from jax.experimental.pallas import tpu as pltpu
from jax.sharding import PartitionSpec as P

HEAD_DIM = 128
BLOCK = 256
ROWS = 64
HEADS = 4
N_TENSOR = 8
N_Y = 4
IN_CHUNKS = (512,) * 6
N_IN = len(IN_CHUNKS)
OUT_CHUNKS = 6
LAG = 3
EARLY = 2
OWN, UP, DOWN, OPPOSITE = range(N_Y)
F32 = jnp.float32
BF16 = jnp.bfloat16


def silu(v):
    half = 0.5 * v
    return half + half * jnp.tanh(half)


def split(n_ctx):
    n_x = 4 if n_ctx > 8 else 2
    n_half = n_ctx // 2
    return n_x, n_ctx // n_x, n_half, HEADS * HEAD_DIM // n_half


def kernel(
    n_ctx, x_ref, w_ref, wo_ref, ld_ref, out_ref,
    xall, wv, w2, acc, qs_s, k_s, v_s, mask_s, eq_s, ek_s, inner_s, u_s,
    ld4, ld8, cum_s, elast_s, dsend, dec, edec,
    st1, rc1, st2, rc2, before, after, nsend, nrm, part, relay, summed, from_b, from_f,
    ag_send, ag_up, ag_down, ag_o, ag_s, ag_so, own_sem, w_sem, wo_own, wo_send, wo_recv,
    dec_send, dec_recv, p1_send, p1_recv, p2_send, p2_recv, n_send, n_recv,
    rs_send, rs_relay, rs_b, rs_f, rs_sum_send, ld_sem, half_send, half_recv, ready,
):
    ctx = lax.axis_index("context")
    t = lax.axis_index("tensor")
    y = t // 2
    core = t % 2
    other = 1 - core
    sib = y * 2 + other
    d_model = x_ref.shape[1]
    nc = d_model // OUT_CHUNKS

    n_x, n_z, n_half, chunk_rows = split(n_ctx)
    half_z = n_z // 2
    half, place = ctx // n_half, ctx % n_half
    first = half * n_half
    partner = (n_z - 1 - ctx // n_x) * n_x + ctx % n_x

    def piece_of(at):
        z = at // n_x
        return (z + half * (half_z - 1 - 2 * z)) * n_x + at % n_x

    piece = piece_of(place)

    others = sorted(
        ((dz, dx) for dz in range(half_z) for dx in range(n_x) if dz or dx),
        key=lambda d: -(2 * min(d[0], 1) + min(d[1], n_x - d[1])),
    )
    peers = [
        (place // n_x + dz) % half_z * n_x + (place % n_x + dx) % n_x for dz, dx in others
    ]

    def remote(src, dst, send, recv, device):
        return pltpu.make_async_remote_copy(
            src_ref=src, dst_ref=dst, send_sem=send, recv_sem=recv,
            device_id=device, device_id_type=pl.DeviceIdType.MESH,
        )

    def ring(j):
        step = 1 - 2 * ((j + core) % 2)
        fwd = (y + step + N_Y) % N_Y
        bwd = (y - step + N_Y) % N_Y
        return fwd, bwd

    def in_cols(j):
        return pl.ds(sum(IN_CHUNKS[:j]), IN_CHUNKS[j])

    def out_cols(j):
        return pl.ds(pl.multiple_of(j * nc, nc), nc)

    def w_copy(j):
        rows = in_cols(j)
        return pltpu.make_async_copy(w_ref.at[:, rows, :], wv.at[:, rows, :], w_sem.at[j])

    def own_copy(j):
        cols = in_cols(j)
        return pltpu.make_async_copy(x_ref.at[:, cols], xall.at[OWN, core, :, cols], own_sem.at[j])

    up, down = (y + 1) % N_Y * 2, (y + N_Y - 1) % N_Y * 2

    def send_own(j):
        cols = in_cols(j)
        src = xall.at[OWN, core, :, cols]
        own_copy(j).wait()
        remote(
            src, xall.at[DOWN, core, :, cols], ag_send, ag_down.at[j], {"tensor": up + core}
        ).start()
        remote(
            src, xall.at[UP, core, :, cols], ag_send, ag_up.at[j], {"tensor": down + core}
        ).start()
        remote(src, src, ag_send, ag_s.at[j], {"tensor": sib}).start()

    def arrived(ref, sem):
        remote(ref, ref, ag_send, sem, {"tensor": sib}).wait_recv()

    def pass_near(j):
        cols = in_cols(j)
        arrived(xall.at[DOWN, core, :, cols], ag_down.at[j])
        arrived(xall.at[UP, core, :, cols], ag_up.at[j])
        upward = (j + core) % 2
        chip = (y + 2 * upward + N_Y - 1) % N_Y * 2
        src = xall.at[UP + upward, core, :, cols]
        dst = xall.at[OPPOSITE, core, :, cols]
        remote(src, dst, ag_send, ag_o.at[j], {"tensor": chip + core}).start()
        if j == N_IN - 1:
            remote(src, dst, ag_send, ag_so.at[j], {"tensor": chip + other}).start()
        near = xall.at[pl.ds(UP, 2), core, :, cols]
        remote(near, near, ag_send, ag_s.at[j], {"tensor": sib}).start()

    def pass_opposite(j):
        ref = xall.at[OPPOSITE, core, :, in_cols(j)]
        arrived(ref, ag_o.at[j])
        if j < N_IN - 1:
            remote(ref, ref, ag_send, ag_so.at[j], {"tensor": sib}).start()

    def multiply(j, slots, parts):
        first, count = slots
        rows = slice(first * 2 * ROWS, (first + count) * 2 * ROWS)
        values = xall[first : first + count, :, :, in_cols(j)].reshape(
            count * 2 * ROWS, IN_CHUNKS[j]
        )
        for i in parts:
            product = jnp.dot(values, wv[i, in_cols(j), :], preferred_element_type=F32)
            acc[i, rows] = product if j == 0 else acc[i, rows] + product

    def multiply_near(j):
        w_copy(j).wait()
        arrived(xall.at[pl.ds(OWN, 3), other, :, in_cols(j)], ag_s.at[j])
        multiply(j, (OWN, 3), (0, 1, 2))

    def multiply_opposite(j):
        arrived(xall.at[OPPOSITE, other, :, in_cols(j)], ag_so.at[j])
        multiply(j, (OPPOSITE, 1), (1, 2))

    def rows_of(i, chip, lanes):
        ahead = (chip - y + N_Y) % N_Y
        slot = ahead + ahead // 2 * (5 - 2 * ahead)
        return acc[i, pl.ds(pl.multiple_of(slot * 2 * ROWS, 2 * ROWS), 2 * ROWS), lanes]

    def block_of(i, n, lanes):
        return jnp.concatenate([rows_of(i, 2 * n, lanes), rows_of(i, 2 * n + 1, lanes)], axis=0)

    ld_copy = pltpu.make_async_copy(ld_ref, ld4, ld_sem)
    ld_copy.start()
    for j in range(N_IN):
        own_copy(j).start()
        w_copy(j).start()
    wo_copy = pltpu.make_async_copy(wo_ref, w2.at[pl.ds(0, HEADS * HEAD_DIM)], wo_own)
    wo_copy.start()

    barrier = pltpu.get_barrier_semaphore()
    for peer in (up + core, down + core, sib, up + other, down + other):
        pl.semaphore_signal(
            barrier, inc=1, device_id={"tensor": peer}, device_id_type=pl.DeviceIdType.MESH
        )

    for to in peers:
        pl.semaphore_signal(
            barrier, inc=1, device_id={"context": first + to},
            device_id_type=pl.DeviceIdType.MESH,
        )

    @pl.when(half == 0)
    def _():
        pl.semaphore_signal(
            barrier, inc=1, device_id={"context": partner}, device_id_type=pl.DeviceIdType.MESH
        )

    pl.semaphore_wait(barrier, 5 + n_half - 1 + half)

    for j in range(N_IN):
        send_own(j)

    @pl.when(half == 1)
    def _():
        pl.semaphore_signal(
            ready, inc=1, device_id={"context": partner}, device_id_type=pl.DeviceIdType.MESH
        )

    @pl.when(half == 0)
    def _():
        before[...] = jnp.zeros_like(before)

    ld_copy.wait()
    ld8[0:HEADS, :] = ld4[:, 0:BLOCK]
    ld8[HEADS : 2 * HEADS, :] = ld4[:, BLOCK : 2 * BLOCK]
    cum = ld8[...]
    lane = lax.broadcasted_iota(jnp.int32, (2 * HEADS, BLOCK), 1)
    shift = 1
    while shift < BLOCK:
        cum = cum + jnp.where(lane >= shift, pltpu.roll(cum, shift, 1), 0.0)
        shift *= 2
    cum_s[...] = cum
    last = jnp.broadcast_to(cum[:, BLOCK - 1 : BLOCK], (2 * HEADS, HEAD_DIM))
    elast_s[...] = jnp.exp(last)
    both = last + pltpu.roll(last, HEADS, 0)
    dsend[...] = both
    dec[pl.ds(place, 1)] = both[None]

    for to in peers:
        remote(dsend, dec.at[place], dec_send, dec_recv, {"context": first + to}).start()

    def decay_tables(r):
        row = cum_s[pl.ds(r, 1), :]
        column = jnp.transpose(jnp.broadcast_to(row, (HEAD_DIM, BLOCK)))
        end = row[:, BLOCK - 1 : BLOCK]
        eq_s[r] = jnp.exp(column).reshape(2, 2, ROWS, HEAD_DIM)
        ek_s[r] = jnp.exp(end - column)
        for half in range(2):
            at = half * HEAD_DIM
            gaps = jnp.minimum(column - row[:, at : at + HEAD_DIM], 0.0)
            i = lax.broadcasted_iota(jnp.int32, (BLOCK, HEAD_DIM), 0)
            k = lax.broadcasted_iota(jnp.int32, (BLOCK, HEAD_DIM), 1) + at
            mask_s[r, :, at : at + HEAD_DIM] = jnp.where(i >= k, jnp.exp(gaps), 0.0)

    for j in range(N_IN + 1):
        if j < N_IN:
            pass_near(j)
        for r in range(2 * HEADS):
            if r * (N_IN + 1) // (2 * HEADS) == j:
                decay_tables(r)
        if j == N_IN:
            for k in range(EARLY):
                pass_opposite(k)
        if j > 0:
            multiply_near(j - 1)

    def decay_size():
        return remote(
            dec.at[pl.ds(0, n_half - 1)], dec.at[pl.ds(0, n_half - 1)],
            dec_send, dec_recv, {"tensor": sib},
        )

    decay_size().wait_recv()
    my_head = piece * chunk_rows // HEAD_DIM
    for i in range(n_half):
        edec[i : i + 1, :] = jnp.exp(dec[i, pl.ds(my_head, 1), :])

    for j in range(EARLY, N_IN + EARLY):
        if j < N_IN:
            pass_opposite(j)
        multiply_opposite(j - EARLY)
    remote(
        wo_ref, w2.at[pl.ds(HEADS * HEAD_DIM, HEADS * HEAD_DIM)],
        wo_send, wo_recv, {"tensor": sib},
    ).start()

    for h in range(HEADS):
        lanes = slice(h * HEAD_DIM, (h + 1) * HEAD_DIM)
        states = []
        for n in range(2):
            rows = slice(n * BLOCK, (n + 1) * BLOCK)
            keys = silu(block_of(1, n, lanes)).astype(BF16)
            values = block_of(2, n, lanes).astype(BF16)
            k_s[h, rows] = keys
            v_s[h, rows] = values
            weighted = (keys.astype(F32) * ek_s[n * HEADS + h]).astype(BF16)
            states.append(
                lax.dot_general(
                    weighted, values, (((0,), (0,)), ((), ())), preferred_element_type=F32
                )
            )
        u_s[h] = states[0]
        total = elast_s[HEADS + h : HEADS + h + 1, :] * states[0] + states[1]
        pieces = HEAD_DIM // chunk_rows
        st1[h * pieces : (h + 1) * pieces] = total.astype(BF16).reshape(
            pieces, chunk_rows, HEAD_DIM
        )

    for to in peers:
        remote(
            st1.at[piece_of(to)], rc1.at[place], p1_send, p1_recv, {"context": first + to}
        ).start()
    rc1[pl.ds(place, 1)] = st1[pl.ds(piece, 1)]

    for j in range(N_IN):
        multiply(j, (OPPOSITE, 1), (0,))

    def attend(n):
        for h in range(HEADS):
            lanes = slice(h * HEAD_DIM, (h + 1) * HEAD_DIM)
            rows = slice(n * BLOCK, (n + 1) * BLOCK)
            queries = silu(block_of(0, n, lanes)).astype(BF16)
            weights = lax.dot_general(
                queries, k_s[h, rows, :], (((1,), (1,)), ((), ())), preferred_element_type=F32
            )
            weights = (weights * mask_s[n * HEADS + h]).astype(BF16)
            inner_s[h, 2 * n : 2 * n + 2] = jnp.dot(
                weights, v_s[h, rows, :], preferred_element_type=F32
            ).reshape(2, 2, ROWS, HEAD_DIM)
            scaled = queries.astype(F32).reshape(2, 2, ROWS, HEAD_DIM) * eq_s[n * HEADS + h]
            qs_s[h, 2 * n : 2 * n + 2] = scaled.astype(BF16)

    attend(0)

    def state_size(buffer, send, recv):
        others_of = buffer.at[pl.ds(0, n_half - 1)]
        return remote(others_of, others_of, send, recv, {"tensor": sib})

    state_size(rc1, p1_send, p1_recv).wait_recv()
    half_copy = remote(after, before, half_send, half_recv, {"context": partner})

    @pl.when(half == 1)
    def _():
        half_copy.wait_recv()

    running = before[...]
    for i in range(n_half):
        st2[i] = running.astype(BF16)
        running = running * edec[i : i + 1, :] + rc1[i].astype(F32)

    @pl.when(half == 0)
    def _():
        after[...] = running
        pl.semaphore_wait(ready, 1)
        half_copy.start()

    for to in peers:
        remote(
            st2.at[to], rc2.at[piece], p2_send, p2_recv, {"context": first + to}
        ).start()
    rc2[pl.ds(piece, 1)] = st2[pl.ds(place, 1)]

    attend(1)

    state_size(rc2, p2_send, p2_recv).wait_recv()

    pieces = HEAD_DIM // chunk_rows

    def normalize(which, target):
        for h in range(HEADS):
            lanes = slice(h * HEAD_DIM, (h + 1) * HEAD_DIM)
            entering = rc2[h * pieces : (h + 1) * pieces].reshape(HEAD_DIM, HEAD_DIM)
            later = elast_s[h : h + 1, :] * entering.astype(F32) + u_s[h]
            for n, state in enumerate((entering, later.astype(BF16))):
                queries = qs_s[h, 2 * n : 2 * n + 2, which].reshape(2 * ROWS, HEAD_DIM)
                attended = inner_s[h, 2 * n : 2 * n + 2, which].reshape(
                    2 * ROWS, HEAD_DIM
                ) + jnp.dot(queries, state, preferred_element_type=F32)
                size = jnp.mean(attended * attended, axis=1, keepdims=True)
                normed = (attended * lax.rsqrt(size + 1e-06)).astype(BF16)
                target[2 * n : 2 * n + 2, :, lanes] = normed.reshape(2, ROWS, HEAD_DIM)

    width = HEADS * HEAD_DIM
    normalize(other, nsend)
    norm_copy = remote(
        nsend, nrm.at[:, :, pl.ds(width, width)], n_send, n_recv, {"tensor": sib}
    )
    norm_copy.start()
    normalize(core, nrm)
    wo_copy.wait()
    w2_half = w2.at[pl.ds(width, width)]
    wo_wait = remote(w2_half, w2_half, wo_send, wo_recv, {"tensor": sib})
    wo_wait.wait_recv()
    norm_copy.wait_recv()

    def project(j):
        cols = out_cols(j)
        rows = nrm[...].reshape(N_Y * ROWS, 2 * width)
        chunk = jnp.dot(rows, w2[:, cols], preferred_element_type=F32).astype(BF16)
        part[:, :, cols] = chunk.reshape(N_Y, ROWS, nc)
        fwd, bwd = ring(j)
        remote(
            part.at[(y + 2) % N_Y, :, cols], relay.at[:, cols],
            rs_send, rs_relay.at[j], {"tensor": fwd * 2 + core},
        ).start()
        remote(
            part.at[bwd, :, cols], from_f.at[:, cols],
            rs_send, rs_f.at[j], {"tensor": bwd * 2 + core},
        ).start()

    def pass_on(j):
        cols = out_cols(j)
        fwd, _ = ring(j)
        remote(
            relay.at[:, cols], relay.at[:, cols], rs_send, rs_relay.at[j], {"tensor": sib}
        ).wait_recv()
        summed[:, cols] = (
            part[pl.ds(fwd, 1), :, cols].reshape(ROWS, nc).astype(F32)
            + relay[:, cols].astype(F32)
        ).astype(BF16)
        remote(
            summed.at[:, cols], from_b.at[:, cols],
            rs_sum_send, rs_b.at[j], {"tensor": fwd * 2 + core},
        ).start()

    def finish_rows(j):
        cols = out_cols(j)
        remote(
            from_f.at[:, cols], from_f.at[:, cols], rs_send, rs_f.at[j], {"tensor": sib}
        ).wait_recv()
        remote(
            from_b.at[:, cols], from_b.at[:, cols], rs_send, rs_b.at[j], {"tensor": sib}
        ).wait_recv()
        out_ref[:, cols] = (
            part[pl.ds(y, 1), :, cols].reshape(ROWS, nc).astype(F32)
            + from_f[:, cols].astype(F32)
            + from_b[:, cols].astype(F32)
        ).astype(out_ref.dtype)

    def project_step(j, carry):
        project(j)

        @pl.when(j >= LAG)
        def _():
            pass_on(j - LAG)

        return carry

    lax.fori_loop(0, OUT_CHUNKS, project_step, 0)

    def pass_step(j, carry):
        pass_on(j)
        finish_rows(j - (OUT_CHUNKS - LAG))
        return carry

    lax.fori_loop(OUT_CHUNKS - LAG, OUT_CHUNKS, pass_step, 0)

    seven = w2.at[pl.ds(0, 7 * ROWS)]
    remote(seven, seven, ag_send, ag_s.at[0], {"tensor": sib}).wait_send()
    wo_wait.wait_send()
    decay_size().wait_send()
    state_size(st1, p1_send, p1_recv).wait_send()
    state_size(st2, p2_send, p2_recv).wait_send()
    norm_copy.wait_send()

    @pl.when(half == 0)
    def _():
        half_copy.wait_send()


    def finish_step(j, carry):
        finish_rows(j)
        return carry

    lax.fori_loop(LAG, OUT_CHUNKS, finish_step, 0)
    two = part.at[pl.ds(0, 2)]
    remote(two, two, rs_send, rs_f.at[0], {"tensor": sib}).wait_send()
    remote(summed, summed, rs_sum_send, rs_b.at[0], {"tensor": sib}).wait_send()


def body(n_ctx, activations, w_qkv, w_out, log_decay):
    rows, d_model = activations.shape
    width = HEADS * HEAD_DIM
    _, _, n_half, chunk_rows = split(n_ctx)
    hbm = pl.BlockSpec(memory_space=pltpu.HBM)
    vmem = pl.BlockSpec(memory_space=pltpu.VMEM)
    dma = pltpu.SemaphoreType.DMA
    shard = N_TENSOR * rows
    scratch = [
        pltpu.VMEM((N_Y, 2, rows, d_model), BF16),
        pltpu.VMEM((3, d_model, width), BF16),
        pltpu.VMEM((2 * width, d_model), BF16),
        pltpu.VMEM((3, shard, width), F32),
        pltpu.VMEM((HEADS, N_Y, 2, rows, HEAD_DIM), BF16),
        pltpu.VMEM((HEADS, shard, HEAD_DIM), BF16),
        pltpu.VMEM((HEADS, shard, HEAD_DIM), BF16),
        pltpu.VMEM((2 * HEADS, BLOCK, BLOCK), F32),
        pltpu.VMEM((2 * HEADS, 2, 2, rows, HEAD_DIM), F32),
        pltpu.VMEM((2 * HEADS, BLOCK, HEAD_DIM), F32),
        pltpu.VMEM((HEADS, N_Y, 2, rows, HEAD_DIM), F32),
        pltpu.VMEM((HEADS, HEAD_DIM, HEAD_DIM), F32),
        pltpu.VMEM((HEADS, 2 * BLOCK), F32),
        pltpu.VMEM((2 * HEADS, BLOCK), F32),
        pltpu.VMEM((2 * HEADS, BLOCK), F32),
        pltpu.VMEM((2 * HEADS, HEAD_DIM), F32),
        pltpu.VMEM((2 * HEADS, HEAD_DIM), F32),
        pltpu.VMEM((n_half, 2 * HEADS, HEAD_DIM), F32),
        pltpu.VMEM((n_half, HEAD_DIM), F32),
        pltpu.VMEM((n_half, chunk_rows, HEAD_DIM), BF16),
        pltpu.VMEM((n_half, chunk_rows, HEAD_DIM), BF16),
        pltpu.VMEM((n_half, chunk_rows, HEAD_DIM), BF16),
        pltpu.VMEM((n_half, chunk_rows, HEAD_DIM), BF16),
        pltpu.VMEM((chunk_rows, HEAD_DIM), F32),
        pltpu.VMEM((chunk_rows, HEAD_DIM), F32),
        pltpu.VMEM((N_Y, rows, width), BF16),
        pltpu.VMEM((N_Y, rows, 2 * width), BF16),
        pltpu.VMEM((N_Y, rows, d_model), BF16),
        pltpu.VMEM((rows, d_model), BF16),
        pltpu.VMEM((rows, d_model), BF16),
        pltpu.VMEM((rows, d_model), BF16),
        pltpu.VMEM((rows, d_model), BF16),
        dma,
        dma((N_IN,)),
        dma((N_IN,)),
        dma((N_IN,)),
        dma((N_IN,)),
        dma((N_IN,)),
        dma((N_IN,)),
        dma((N_IN,)),
        dma,
        dma,
        dma,
        dma,
        dma,
        dma,
        dma,
        dma,
        dma,
        dma,
        dma,
        dma,
        dma((OUT_CHUNKS,)),
        dma((OUT_CHUNKS,)),
        dma((OUT_CHUNKS,)),
        dma,
        dma,
        dma,
        dma,
        pltpu.SemaphoreType.REGULAR,
    ]
    return pl.pallas_call(
        functools.partial(kernel, n_ctx),
        out_shape=jax.ShapeDtypeStruct((rows, d_model), BF16),
        in_specs=[hbm, hbm, hbm, hbm],
        out_specs=vmem,
        scratch_shapes=scratch,
        compiler_params=pltpu.CompilerParams(
            collective_id=0, has_side_effects=True, vmem_limit_bytes=52 * 1024 * 1024
        ),
    )(*(
        pltpu.with_memory_space_constraint(array, pltpu.HBM)
        for array in (activations, w_qkv.transpose(1, 0, 2), w_out, log_decay)
    ))


def solution(mesh):
    in_specs = (
        P(("context", "tensor"), None),
        P(None, None, "tensor"),
        P("tensor", None),
        P("tensor", "context"),
    )
    out_specs = P(("context", "tensor"), None)
    return jax.shard_map(
        functools.partial(body, mesh.shape["context"]),
        mesh=mesh, in_specs=in_specs, out_specs=out_specs, check_vma=False,
    )
```

```python
import functools

import jax
import jax.numpy as jnp
from jax import lax
from jax.experimental import pallas as pl
from jax.experimental.pallas import tpu as pltpu
from jax.sharding import PartitionSpec as P

HEAD_DIM = 128
BLOCK = 256
ROWS = 64
HEADS = 4
N_TENSOR = 8
N_X = 4
N_Y = 4
GROUPS = 4
IN_CHUNKS = (512,) * 6
N_IN = len(IN_CHUNKS)
OUT_CHUNKS = 6
LAG = 3
EARLY = 2
OWN, UP, DOWN, OPPOSITE = range(N_Y)
F32 = jnp.float32
BF16 = jnp.bfloat16


def silu(v):
    half = 0.5 * v
    return half + half * jnp.tanh(half)


def split(n_ctx):
    n_in = n_ctx // GROUPS
    return n_in, HEADS * HEAD_DIM // n_in


def kernel(
    n_ctx, x_ref, w_ref, wo_ref, ld_ref, out_ref,
    xall, wv, w2, acc, qs_s, k_s, v_s, mask_s, eq_s, ek_s, inner_s, u_s,
    ld4, ld8, cum_s, elast_s, dsend, dec, edec,
    st1, rc1, st2, rc2, before, after, nsend, nrm, part, relay, summed, from_b, from_f,
    ag_send, ag_up, ag_down, ag_o, ag_s, ag_so, own_sem, w_sem, wo_own, wo_send, wo_recv,
    dec_send, dec_recv, p1_send, p1_recv, p2_send, p2_recv, n_send, n_recv,
    rs_send, rs_relay, rs_b, rs_f, rs_sum_send, ld_sem, group_send, group_recv, ready,
):
    ctx = lax.axis_index("context")
    t = lax.axis_index("tensor")
    y = t // 2
    core = t % 2
    other = 1 - core
    sib = y * 2 + other
    d_model = x_ref.shape[1]
    nc = d_model // OUT_CHUNKS

    n_in, chunk_rows = split(n_ctx)
    group, place = ctx // n_in, ctx % n_in
    first = group * n_in

    others = sorted(
        ((dz, dx) for dz in range(n_in // N_X) for dx in range(N_X) if dz or dx),
        key=lambda d: -(d[0] + min(d[1], N_X - d[1])),
    )
    peers = [
        (place // N_X + dz) % (n_in // N_X) * N_X + (place % N_X + dx) % N_X
        for dz, dx in others
    ]

    def remote(src, dst, send, recv, device):
        return pltpu.make_async_remote_copy(
            src_ref=src, dst_ref=dst, send_sem=send, recv_sem=recv,
            device_id=device, device_id_type=pl.DeviceIdType.MESH,
        )

    def ring(j):
        step = 1 - 2 * ((j + core) % 2)
        fwd = (y + step + N_Y) % N_Y
        bwd = (y - step + N_Y) % N_Y
        return fwd, bwd

    def in_cols(j):
        return pl.ds(sum(IN_CHUNKS[:j]), IN_CHUNKS[j])

    def out_cols(j):
        return pl.ds(pl.multiple_of(j * nc, nc), nc)

    def w_copy(j):
        rows = in_cols(j)
        return pltpu.make_async_copy(w_ref.at[:, rows, :], wv.at[:, rows, :], w_sem.at[j])

    def own_copy(j):
        cols = in_cols(j)
        return pltpu.make_async_copy(x_ref.at[:, cols], xall.at[OWN, core, :, cols], own_sem.at[j])

    up, down = (y + 1) % N_Y * 2, (y + N_Y - 1) % N_Y * 2

    def send_own(j):
        cols = in_cols(j)
        src = xall.at[OWN, core, :, cols]
        own_copy(j).wait()
        remote(
            src, xall.at[DOWN, core, :, cols], ag_send, ag_down.at[j], {"tensor": up + core}
        ).start()
        remote(
            src, xall.at[UP, core, :, cols], ag_send, ag_up.at[j], {"tensor": down + core}
        ).start()
        remote(src, src, ag_send, ag_s.at[j], {"tensor": sib}).start()

    def arrived(ref, sem):
        remote(ref, ref, ag_send, sem, {"tensor": sib}).wait_recv()

    def pass_near(j):
        cols = in_cols(j)
        arrived(xall.at[DOWN, core, :, cols], ag_down.at[j])
        arrived(xall.at[UP, core, :, cols], ag_up.at[j])
        upward = (j + core) % 2
        chip = (y + 2 * upward + N_Y - 1) % N_Y * 2
        src = xall.at[UP + upward, core, :, cols]
        dst = xall.at[OPPOSITE, core, :, cols]
        remote(src, dst, ag_send, ag_o.at[j], {"tensor": chip + core}).start()
        if j == N_IN - 1:
            remote(src, dst, ag_send, ag_so.at[j], {"tensor": chip + other}).start()
        near = xall.at[pl.ds(UP, 2), core, :, cols]
        remote(near, near, ag_send, ag_s.at[j], {"tensor": sib}).start()

    def pass_opposite(j):
        ref = xall.at[OPPOSITE, core, :, in_cols(j)]
        arrived(ref, ag_o.at[j])
        if j < N_IN - 1:
            remote(ref, ref, ag_send, ag_so.at[j], {"tensor": sib}).start()

    def multiply(j, slots, parts):
        first, count = slots
        rows = slice(first * 2 * ROWS, (first + count) * 2 * ROWS)
        values = xall[first : first + count, :, :, in_cols(j)].reshape(
            count * 2 * ROWS, IN_CHUNKS[j]
        )
        for i in parts:
            product = jnp.dot(values, wv[i, in_cols(j), :], preferred_element_type=F32)
            acc[i, rows] = product if j == 0 else acc[i, rows] + product

    def multiply_near(j):
        w_copy(j).wait()
        arrived(xall.at[pl.ds(OWN, 3), other, :, in_cols(j)], ag_s.at[j])
        multiply(j, (OWN, 3), (0, 1, 2))

    def multiply_opposite(j):
        arrived(xall.at[OPPOSITE, other, :, in_cols(j)], ag_so.at[j])
        multiply(j, (OPPOSITE, 1), (1, 2))

    def rows_of(i, chip, lanes):
        ahead = (chip - y + N_Y) % N_Y
        slot = ahead + ahead // 2 * (5 - 2 * ahead)
        return acc[i, pl.ds(pl.multiple_of(slot * 2 * ROWS, 2 * ROWS), 2 * ROWS), lanes]

    def block_of(i, n, lanes):
        return jnp.concatenate([rows_of(i, 2 * n, lanes), rows_of(i, 2 * n + 1, lanes)], axis=0)

    ld_copy = pltpu.make_async_copy(ld_ref, ld4, ld_sem)
    ld_copy.start()
    for j in range(N_IN):
        own_copy(j).start()
        w_copy(j).start()
    wo_copy = pltpu.make_async_copy(wo_ref, w2.at[pl.ds(0, HEADS * HEAD_DIM)], wo_own)
    wo_copy.start()

    barrier = pltpu.get_barrier_semaphore()
    for peer in (up + core, down + core, sib, up + other, down + other):
        pl.semaphore_signal(
            barrier, inc=1, device_id={"tensor": peer}, device_id_type=pl.DeviceIdType.MESH
        )

    for to in peers:
        pl.semaphore_signal(
            barrier, inc=1, device_id={"context": first + to},
            device_id_type=pl.DeviceIdType.MESH,
        )

    for later_group in range(1, GROUPS):
        @pl.when(later_group > group)
        def _():
            pl.semaphore_signal(
                barrier, inc=1, device_id={"context": later_group * n_in + place},
                device_id_type=pl.DeviceIdType.MESH,
            )

    pl.semaphore_wait(barrier, 5 + n_in - 1 + group)

    for j in range(N_IN):
        send_own(j)

    for earlier in range(GROUPS - 1):
        @pl.when(earlier < group)
        def _():
            pl.semaphore_signal(
                ready.at[group], inc=1, device_id={"context": earlier * n_in + place},
                device_id_type=pl.DeviceIdType.MESH,
            )

        @pl.when(earlier >= group)
        def _():
            before[earlier, 0:chunk_rows] = jnp.zeros((chunk_rows, HEAD_DIM), F32)
            before[earlier, chunk_rows:] = jnp.ones((8, HEAD_DIM), F32)

    ld_copy.wait()
    ld8[0:HEADS, :] = ld4[:, 0:BLOCK]
    ld8[HEADS : 2 * HEADS, :] = ld4[:, BLOCK : 2 * BLOCK]
    cum = ld8[...]
    lane = lax.broadcasted_iota(jnp.int32, (2 * HEADS, BLOCK), 1)
    shift = 1
    while shift < BLOCK:
        cum = cum + jnp.where(lane >= shift, pltpu.roll(cum, shift, 1), 0.0)
        shift *= 2
    cum_s[...] = cum
    last = jnp.broadcast_to(cum[:, BLOCK - 1 : BLOCK], (2 * HEADS, HEAD_DIM))
    elast_s[...] = jnp.exp(last)
    both = last + pltpu.roll(last, HEADS, 0)
    dsend[...] = both
    dec[pl.ds(place, 1)] = both[None]

    for to in peers:
        remote(dsend, dec.at[place], dec_send, dec_recv, {"context": first + to}).start()

    def decay_tables(r):
        row = cum_s[pl.ds(r, 1), :]
        column = jnp.transpose(jnp.broadcast_to(row, (HEAD_DIM, BLOCK)))
        end = row[:, BLOCK - 1 : BLOCK]
        eq_s[r] = jnp.exp(column).reshape(2, 2, ROWS, HEAD_DIM)
        ek_s[r] = jnp.exp(end - column)
        for half in range(2):
            at = half * HEAD_DIM
            gaps = jnp.minimum(column - row[:, at : at + HEAD_DIM], 0.0)
            i = lax.broadcasted_iota(jnp.int32, (BLOCK, HEAD_DIM), 0)
            k = lax.broadcasted_iota(jnp.int32, (BLOCK, HEAD_DIM), 1) + at
            mask_s[r, :, at : at + HEAD_DIM] = jnp.where(i >= k, jnp.exp(gaps), 0.0)

    for j in range(N_IN + 1):
        if j < N_IN:
            pass_near(j)
        for r in range(2 * HEADS):
            if r * (N_IN + 1) // (2 * HEADS) == j:
                decay_tables(r)
        if j == N_IN:
            for k in range(EARLY):
                pass_opposite(k)
        if j > 0:
            multiply_near(j - 1)

    def decay_size():
        return remote(
            dec.at[pl.ds(0, n_in - 1)], dec.at[pl.ds(0, n_in - 1)],
            dec_send, dec_recv, {"tensor": sib},
        )

    decay_size().wait_recv()
    my_head = place * chunk_rows // HEAD_DIM
    for i in range(n_in):
        edec[i : i + 1, :] = jnp.exp(dec[i, pl.ds(my_head, 1), :])

    for j in range(EARLY, N_IN + EARLY):
        if j < N_IN:
            pass_opposite(j)
        multiply_opposite(j - EARLY)
    remote(
        wo_ref, w2.at[pl.ds(HEADS * HEAD_DIM, HEADS * HEAD_DIM)],
        wo_send, wo_recv, {"tensor": sib},
    ).start()

    for h in range(HEADS):
        lanes = slice(h * HEAD_DIM, (h + 1) * HEAD_DIM)
        states = []
        for n in range(2):
            rows = slice(n * BLOCK, (n + 1) * BLOCK)
            keys = silu(block_of(1, n, lanes)).astype(BF16)
            values = block_of(2, n, lanes).astype(BF16)
            k_s[h, rows] = keys
            v_s[h, rows] = values
            weighted = (keys.astype(F32) * ek_s[n * HEADS + h]).astype(BF16)
            states.append(
                lax.dot_general(
                    weighted, values, (((0,), (0,)), ((), ())), preferred_element_type=F32
                )
            )
        u_s[h] = states[0]
        total = elast_s[HEADS + h : HEADS + h + 1, :] * states[0] + states[1]
        pieces = HEAD_DIM // chunk_rows
        st1[h * pieces : (h + 1) * pieces] = total.astype(BF16).reshape(
            pieces, chunk_rows, HEAD_DIM
        )

    for to in peers:
        remote(
            st1.at[to], rc1.at[place], p1_send, p1_recv, {"context": first + to}
        ).start()
    rc1[pl.ds(place, 1)] = st1[pl.ds(place, 1)]

    for j in range(N_IN):
        multiply(j, (OPPOSITE, 1), (0,))

    def attend(n):
        for h in range(HEADS):
            lanes = slice(h * HEAD_DIM, (h + 1) * HEAD_DIM)
            rows = slice(n * BLOCK, (n + 1) * BLOCK)
            queries = silu(block_of(0, n, lanes)).astype(BF16)
            weights = lax.dot_general(
                queries, k_s[h, rows, :], (((1,), (1,)), ((), ())), preferred_element_type=F32
            )
            weights = (weights * mask_s[n * HEADS + h]).astype(BF16)
            inner_s[h, 2 * n : 2 * n + 2] = jnp.dot(
                weights, v_s[h, rows, :], preferred_element_type=F32
            ).reshape(2, 2, ROWS, HEAD_DIM)
            scaled = queries.astype(F32).reshape(2, 2, ROWS, HEAD_DIM) * eq_s[n * HEADS + h]
            qs_s[h, 2 * n : 2 * n + 2] = scaled.astype(BF16)

    attend(0)

    def state_size(buffer, send, recv):
        others_of = buffer.at[pl.ds(0, n_in - 1)]
        return remote(others_of, others_of, send, recv, {"tensor": sib})

    state_size(rc1, p1_send, p1_recv).wait_recv()
    def group_copy(to):
        return remote(
            after, before.at[group], group_send.at[to], group_recv.at[group],
            {"context": to * n_in + place},
        )

    running = jnp.zeros((chunk_rows, HEAD_DIM), F32)
    kept = jnp.ones((8, HEAD_DIM), F32)
    for i in range(n_in):
        running = running * edec[i : i + 1, :] + rc1[i].astype(F32)
        kept = kept * edec[i : i + 1, :]
    after[0:chunk_rows] = running
    after[chunk_rows:] = kept
    for later_group in range(1, GROUPS):
        @pl.when(later_group > group)
        def _():
            pl.semaphore_wait(ready.at[later_group], 1)
            group_copy(later_group).start()

    running = jnp.zeros((chunk_rows, HEAD_DIM), F32)
    for earlier in range(GROUPS - 1):
        @pl.when(earlier < group)
        def _():
            remote(
                before.at[earlier], before.at[earlier], group_send.at[0],
                group_recv.at[earlier], {"tensor": sib},
            ).wait_recv()

        running = running * before[earlier, chunk_rows : chunk_rows + 1] + before[
            earlier, 0:chunk_rows
        ]
    for i in range(n_in):
        st2[i] = running.astype(BF16)
        running = running * edec[i : i + 1, :] + rc1[i].astype(F32)
    for to in peers:
        remote(
            st2.at[to], rc2.at[place], p2_send, p2_recv, {"context": first + to}
        ).start()
    rc2[pl.ds(place, 1)] = st2[pl.ds(place, 1)]

    attend(1)

    state_size(rc2, p2_send, p2_recv).wait_recv()

    pieces = HEAD_DIM // chunk_rows

    def normalize(which, target):
        for h in range(HEADS):
            lanes = slice(h * HEAD_DIM, (h + 1) * HEAD_DIM)
            entering = rc2[h * pieces : (h + 1) * pieces].reshape(HEAD_DIM, HEAD_DIM)
            later = elast_s[h : h + 1, :] * entering.astype(F32) + u_s[h]
            for n, state in enumerate((entering, later.astype(BF16))):
                queries = qs_s[h, 2 * n : 2 * n + 2, which].reshape(2 * ROWS, HEAD_DIM)
                attended = inner_s[h, 2 * n : 2 * n + 2, which].reshape(
                    2 * ROWS, HEAD_DIM
                ) + jnp.dot(queries, state, preferred_element_type=F32)
                size = jnp.mean(attended * attended, axis=1, keepdims=True)
                normed = (attended * lax.rsqrt(size + 1e-06)).astype(BF16)
                target[2 * n : 2 * n + 2, :, lanes] = normed.reshape(2, ROWS, HEAD_DIM)

    width = HEADS * HEAD_DIM
    normalize(other, nsend)
    norm_copy = remote(
        nsend, nrm.at[:, :, pl.ds(width, width)], n_send, n_recv, {"tensor": sib}
    )
    norm_copy.start()
    normalize(core, nrm)
    wo_copy.wait()
    w2_half = w2.at[pl.ds(width, width)]
    wo_wait = remote(w2_half, w2_half, wo_send, wo_recv, {"tensor": sib})
    wo_wait.wait_recv()
    norm_copy.wait_recv()

    def project(j):
        cols = out_cols(j)
        rows = nrm[...].reshape(N_Y * ROWS, 2 * width)
        chunk = jnp.dot(rows, w2[:, cols], preferred_element_type=F32).astype(BF16)
        part[:, :, cols] = chunk.reshape(N_Y, ROWS, nc)
        fwd, bwd = ring(j)
        remote(
            part.at[(y + 2) % N_Y, :, cols], relay.at[:, cols],
            rs_send, rs_relay.at[j], {"tensor": fwd * 2 + core},
        ).start()
        remote(
            part.at[bwd, :, cols], from_f.at[:, cols],
            rs_send, rs_f.at[j], {"tensor": bwd * 2 + core},
        ).start()

    def pass_on(j):
        cols = out_cols(j)
        fwd, _ = ring(j)
        remote(
            relay.at[:, cols], relay.at[:, cols], rs_send, rs_relay.at[j], {"tensor": sib}
        ).wait_recv()
        summed[:, cols] = (
            part[pl.ds(fwd, 1), :, cols].reshape(ROWS, nc).astype(F32)
            + relay[:, cols].astype(F32)
        ).astype(BF16)
        remote(
            summed.at[:, cols], from_b.at[:, cols],
            rs_sum_send, rs_b.at[j], {"tensor": fwd * 2 + core},
        ).start()

    def finish_rows(j):
        cols = out_cols(j)
        remote(
            from_f.at[:, cols], from_f.at[:, cols], rs_send, rs_f.at[j], {"tensor": sib}
        ).wait_recv()
        remote(
            from_b.at[:, cols], from_b.at[:, cols], rs_send, rs_b.at[j], {"tensor": sib}
        ).wait_recv()
        out_ref[:, cols] = (
            part[pl.ds(y, 1), :, cols].reshape(ROWS, nc).astype(F32)
            + from_f[:, cols].astype(F32)
            + from_b[:, cols].astype(F32)
        ).astype(out_ref.dtype)

    def project_step(j, carry):
        project(j)

        @pl.when(j >= LAG)
        def _():
            pass_on(j - LAG)

        return carry

    lax.fori_loop(0, OUT_CHUNKS, project_step, 0)

    def pass_step(j, carry):
        pass_on(j)
        finish_rows(j - (OUT_CHUNKS - LAG))
        return carry

    lax.fori_loop(OUT_CHUNKS - LAG, OUT_CHUNKS, pass_step, 0)

    seven = w2.at[pl.ds(0, 7 * ROWS)]
    remote(seven, seven, ag_send, ag_s.at[0], {"tensor": sib}).wait_send()
    wo_wait.wait_send()
    decay_size().wait_send()
    state_size(st1, p1_send, p1_recv).wait_send()
    state_size(st2, p2_send, p2_recv).wait_send()
    norm_copy.wait_send()

    for later_group in range(1, GROUPS):
        @pl.when(later_group > group)
        def _():
            group_copy(later_group).wait_send()


    def finish_step(j, carry):
        finish_rows(j)
        return carry

    lax.fori_loop(LAG, OUT_CHUNKS, finish_step, 0)
    two = part.at[pl.ds(0, 2)]
    remote(two, two, rs_send, rs_f.at[0], {"tensor": sib}).wait_send()
    remote(summed, summed, rs_sum_send, rs_b.at[0], {"tensor": sib}).wait_send()


def body(n_ctx, activations, w_qkv, w_out, log_decay):
    rows, d_model = activations.shape
    width = HEADS * HEAD_DIM
    n_in, chunk_rows = split(n_ctx)
    hbm = pl.BlockSpec(memory_space=pltpu.HBM)
    vmem = pl.BlockSpec(memory_space=pltpu.VMEM)
    dma = pltpu.SemaphoreType.DMA
    shard = N_TENSOR * rows
    scratch = [
        pltpu.VMEM((N_Y, 2, rows, d_model), BF16),
        pltpu.VMEM((3, d_model, width), BF16),
        pltpu.VMEM((2 * width, d_model), BF16),
        pltpu.VMEM((3, shard, width), F32),
        pltpu.VMEM((HEADS, N_Y, 2, rows, HEAD_DIM), BF16),
        pltpu.VMEM((HEADS, shard, HEAD_DIM), BF16),
        pltpu.VMEM((HEADS, shard, HEAD_DIM), BF16),
        pltpu.VMEM((2 * HEADS, BLOCK, BLOCK), F32),
        pltpu.VMEM((2 * HEADS, 2, 2, rows, HEAD_DIM), F32),
        pltpu.VMEM((2 * HEADS, BLOCK, HEAD_DIM), F32),
        pltpu.VMEM((HEADS, N_Y, 2, rows, HEAD_DIM), F32),
        pltpu.VMEM((HEADS, HEAD_DIM, HEAD_DIM), F32),
        pltpu.VMEM((HEADS, 2 * BLOCK), F32),
        pltpu.VMEM((2 * HEADS, BLOCK), F32),
        pltpu.VMEM((2 * HEADS, BLOCK), F32),
        pltpu.VMEM((2 * HEADS, HEAD_DIM), F32),
        pltpu.VMEM((2 * HEADS, HEAD_DIM), F32),
        pltpu.VMEM((n_in, 2 * HEADS, HEAD_DIM), F32),
        pltpu.VMEM((n_in, HEAD_DIM), F32),
        pltpu.VMEM((n_in, chunk_rows, HEAD_DIM), BF16),
        pltpu.VMEM((n_in, chunk_rows, HEAD_DIM), BF16),
        pltpu.VMEM((n_in, chunk_rows, HEAD_DIM), BF16),
        pltpu.VMEM((n_in, chunk_rows, HEAD_DIM), BF16),
        pltpu.VMEM((GROUPS - 1, chunk_rows + 8, HEAD_DIM), F32),
        pltpu.VMEM((chunk_rows + 8, HEAD_DIM), F32),
        pltpu.VMEM((N_Y, rows, width), BF16),
        pltpu.VMEM((N_Y, rows, 2 * width), BF16),
        pltpu.VMEM((N_Y, rows, d_model), BF16),
        pltpu.VMEM((rows, d_model), BF16),
        pltpu.VMEM((rows, d_model), BF16),
        pltpu.VMEM((rows, d_model), BF16),
        pltpu.VMEM((rows, d_model), BF16),
        dma,
        dma((N_IN,)),
        dma((N_IN,)),
        dma((N_IN,)),
        dma((N_IN,)),
        dma((N_IN,)),
        dma((N_IN,)),
        dma((N_IN,)),
        dma,
        dma,
        dma,
        dma,
        dma,
        dma,
        dma,
        dma,
        dma,
        dma,
        dma,
        dma,
        dma((OUT_CHUNKS,)),
        dma((OUT_CHUNKS,)),
        dma((OUT_CHUNKS,)),
        dma,
        dma,
        dma((GROUPS,)),
        dma((GROUPS,)),
        pltpu.SemaphoreType.REGULAR((GROUPS,)),
    ]
    return pl.pallas_call(
        functools.partial(kernel, n_ctx),
        out_shape=jax.ShapeDtypeStruct((rows, d_model), BF16),
        in_specs=[hbm, hbm, hbm, hbm],
        out_specs=vmem,
        scratch_shapes=scratch,
        compiler_params=pltpu.CompilerParams(
            collective_id=0, has_side_effects=True, vmem_limit_bytes=52 * 1024 * 1024
        ),
    )(*(
        pltpu.with_memory_space_constraint(array, pltpu.HBM)
        for array in (activations, w_qkv.transpose(1, 0, 2), w_out, log_decay)
    ))


def solution(mesh):
    in_specs = (
        P(("context", "tensor"), None),
        P(None, None, "tensor"),
        P("tensor", None),
        P("tensor", "context"),
    )
    out_specs = P(("context", "tensor"), None)
    return jax.shard_map(
        functools.partial(body, mesh.shape["context"]),
        mesh=mesh, in_specs=in_specs, out_specs=out_specs, check_vma=False,
    )
```

```python
import functools

import jax
import jax.numpy as jnp
from jax import lax
from jax.experimental import pallas as pl
from jax.experimental.pallas import tpu as pltpu
from jax.sharding import PartitionSpec as P

HEAD_DIM = 128
BLOCK = 256
ROWS = 64
HEADS = 4
N_TENSOR = 8
N_X = 4
N_Y = 4
GROUPS = 4
IN_CHUNKS = (512,) * 6
N_IN = len(IN_CHUNKS)
OUT_CHUNKS = 6
LAG = 3
EARLY = 2
OWN, UP, DOWN, OPPOSITE = range(N_Y)
F32 = jnp.float32
BF16 = jnp.bfloat16


def silu(v):
    half = 0.5 * v
    return half + half * jnp.tanh(half)


def split(n_ctx):
    n_in = n_ctx // GROUPS
    return n_in, HEADS * HEAD_DIM // n_in


def kernel(
    n_ctx, x_ref, w_ref, wo_ref, ld_ref, out_ref,
    xall, wv, w2, acc, qs_s, k_s, v_s, mask_s, eq_s, ek_s, inner_s, u_s,
    ld4, ld8, cum_s, elast_s, dsend, dec, edec,
    st1, rc1, st2, rc2, before, after, nsend, nrm, part, relay, summed, from_b, from_f,
    ag_send, ag_up, ag_down, ag_o, ag_s, ag_so, own_sem, w_sem, wo_own, wo_send, wo_recv,
    dec_send, dec_recv, p1_send, p1_recv, p2_send, p2_recv, n_send, n_recv,
    rs_send, rs_relay, rs_b, rs_f, rs_sum_send, ld_sem, group_send, group_recv, ready,
):
    ctx = lax.axis_index("context")
    t = lax.axis_index("tensor")
    y = t // 2
    core = t % 2
    other = 1 - core
    sib = y * 2 + other
    d_model = x_ref.shape[1]
    nc = d_model // OUT_CHUNKS

    n_in, chunk_rows = split(n_ctx)
    group, place = ctx // n_in, ctx % n_in
    first = group * n_in

    others = sorted(
        ((dz, dx) for dz in range(n_in // N_X) for dx in range(N_X) if dz or dx),
        key=lambda d: -(d[0] + min(d[1], N_X - d[1])),
    )
    peers = [
        (place // N_X + dz) % (n_in // N_X) * N_X + (place % N_X + dx) % N_X
        for dz, dx in others
    ]

    def remote(src, dst, send, recv, device):
        return pltpu.make_async_remote_copy(
            src_ref=src, dst_ref=dst, send_sem=send, recv_sem=recv,
            device_id=device, device_id_type=pl.DeviceIdType.MESH,
        )

    def ring(j):
        step = 1 - 2 * ((j + core) % 2)
        fwd = (y + step + N_Y) % N_Y
        bwd = (y - step + N_Y) % N_Y
        return fwd, bwd

    def in_cols(j):
        return pl.ds(sum(IN_CHUNKS[:j]), IN_CHUNKS[j])

    def out_cols(j):
        return pl.ds(pl.multiple_of(j * nc, nc), nc)

    def w_copy(j):
        rows = in_cols(j)
        return pltpu.make_async_copy(w_ref.at[:, rows, :], wv.at[:, rows, :], w_sem.at[j])

    def own_copy(j):
        cols = in_cols(j)
        return pltpu.make_async_copy(x_ref.at[:, cols], xall.at[OWN, core, :, cols], own_sem.at[j])

    up, down = (y + 1) % N_Y * 2, (y + N_Y - 1) % N_Y * 2

    def send_own(j):
        cols = in_cols(j)
        src = xall.at[OWN, core, :, cols]
        own_copy(j).wait()
        remote(
            src, xall.at[DOWN, core, :, cols], ag_send, ag_down.at[j], {"tensor": up + core}
        ).start()
        remote(
            src, xall.at[UP, core, :, cols], ag_send, ag_up.at[j], {"tensor": down + core}
        ).start()
        remote(src, src, ag_send, ag_s.at[j], {"tensor": sib}).start()

    def arrived(ref, sem):
        remote(ref, ref, ag_send, sem, {"tensor": sib}).wait_recv()

    def pass_near(j):
        cols = in_cols(j)
        arrived(xall.at[DOWN, core, :, cols], ag_down.at[j])
        arrived(xall.at[UP, core, :, cols], ag_up.at[j])
        upward = (j + core) % 2
        chip = (y + 2 * upward + N_Y - 1) % N_Y * 2
        src = xall.at[UP + upward, core, :, cols]
        dst = xall.at[OPPOSITE, core, :, cols]
        remote(src, dst, ag_send, ag_o.at[j], {"tensor": chip + core}).start()
        if j == N_IN - 1:
            remote(src, dst, ag_send, ag_so.at[j], {"tensor": chip + other}).start()
        near = xall.at[pl.ds(UP, 2), core, :, cols]
        remote(near, near, ag_send, ag_s.at[j], {"tensor": sib}).start()

    def pass_opposite(j):
        ref = xall.at[OPPOSITE, core, :, in_cols(j)]
        arrived(ref, ag_o.at[j])
        if j < N_IN - 1:
            remote(ref, ref, ag_send, ag_so.at[j], {"tensor": sib}).start()

    def multiply(j, slots, parts):
        first, count = slots
        rows = slice(first * 2 * ROWS, (first + count) * 2 * ROWS)
        values = xall[first : first + count, :, :, in_cols(j)].reshape(
            count * 2 * ROWS, IN_CHUNKS[j]
        )
        for i in parts:
            product = jnp.dot(values, wv[i, in_cols(j), :], preferred_element_type=F32)
            acc[i, rows] = product if j == 0 else acc[i, rows] + product

    def multiply_near(j):
        w_copy(j).wait()
        arrived(xall.at[pl.ds(OWN, 3), other, :, in_cols(j)], ag_s.at[j])
        multiply(j, (OWN, 3), (0, 1, 2))

    def multiply_opposite(j):
        arrived(xall.at[OPPOSITE, other, :, in_cols(j)], ag_so.at[j])
        multiply(j, (OPPOSITE, 1), (1, 2))

    def rows_of(i, chip, lanes):
        ahead = (chip - y + N_Y) % N_Y
        slot = ahead + ahead // 2 * (5 - 2 * ahead)
        return acc[i, pl.ds(pl.multiple_of(slot * 2 * ROWS, 2 * ROWS), 2 * ROWS), lanes]

    def block_of(i, n, lanes):
        return jnp.concatenate([rows_of(i, 2 * n, lanes), rows_of(i, 2 * n + 1, lanes)], axis=0)

    def two_parts(value):
        high = value.astype(BF16).astype(F32)
        row = lax.broadcasted_iota(jnp.int32, (16, HEAD_DIM), 0)
        return jnp.where(row < 8, high, value - high).astype(BF16)

    ld_copy = pltpu.make_async_copy(ld_ref, ld4, ld_sem)
    ld_copy.start()
    for j in range(N_IN):
        own_copy(j).start()
        w_copy(j).start()
    wo_copy = pltpu.make_async_copy(wo_ref, w2.at[pl.ds(0, HEADS * HEAD_DIM)], wo_own)
    wo_copy.start()

    barrier = pltpu.get_barrier_semaphore()
    for peer in (up + core, down + core, sib, up + other, down + other):
        pl.semaphore_signal(
            barrier, inc=1, device_id={"tensor": peer}, device_id_type=pl.DeviceIdType.MESH
        )

    for to in peers:
        pl.semaphore_signal(
            barrier, inc=1, device_id={"context": first + to},
            device_id_type=pl.DeviceIdType.MESH,
        )

    for later_group in range(1, GROUPS):
        @pl.when(later_group > group)
        def _():
            pl.semaphore_signal(
                barrier, inc=1, device_id={"context": later_group * n_in + place},
                device_id_type=pl.DeviceIdType.MESH,
            )

    pl.semaphore_wait(barrier, 5 + n_in - 1 + group)

    for j in range(N_IN):
        send_own(j)

    for earlier in range(GROUPS - 1):
        @pl.when(earlier < group)
        def _():
            pl.semaphore_signal(
                ready.at[group], inc=1, device_id={"context": earlier * n_in + place},
                device_id_type=pl.DeviceIdType.MESH,
            )

        @pl.when(earlier >= group)
        def _():
            before[earlier, 0:chunk_rows] = jnp.zeros((chunk_rows, HEAD_DIM), BF16)
            before[earlier, chunk_rows:] = two_parts(jnp.ones((16, HEAD_DIM), F32))

    ld_copy.wait()
    ld8[0:HEADS, :] = ld4[:, 0:BLOCK]
    ld8[HEADS : 2 * HEADS, :] = ld4[:, BLOCK : 2 * BLOCK]
    cum = ld8[...]
    lane = lax.broadcasted_iota(jnp.int32, (2 * HEADS, BLOCK), 1)
    shift = 1
    while shift < BLOCK:
        cum = cum + jnp.where(lane >= shift, pltpu.roll(cum, shift, 1), 0.0)
        shift *= 2
    cum_s[...] = cum
    last = jnp.broadcast_to(cum[:, BLOCK - 1 : BLOCK], (2 * HEADS, HEAD_DIM))
    elast_s[...] = jnp.exp(last)
    both = last + pltpu.roll(last, HEADS, 0)
    dsend[...] = both
    dec[pl.ds(place, 1)] = both[None]

    for to in peers:
        remote(dsend, dec.at[place], dec_send, dec_recv, {"context": first + to}).start()

    def decay_tables(r):
        row = cum_s[pl.ds(r, 1), :]
        column = jnp.transpose(jnp.broadcast_to(row, (HEAD_DIM, BLOCK)))
        end = row[:, BLOCK - 1 : BLOCK]
        eq_s[r] = jnp.exp(column).reshape(2, 2, ROWS, HEAD_DIM)
        ek_s[r] = jnp.exp(end - column)
        for half in range(2):
            at = half * HEAD_DIM
            gaps = jnp.minimum(column - row[:, at : at + HEAD_DIM], 0.0)
            i = lax.broadcasted_iota(jnp.int32, (BLOCK, HEAD_DIM), 0)
            k = lax.broadcasted_iota(jnp.int32, (BLOCK, HEAD_DIM), 1) + at
            mask_s[r, :, at : at + HEAD_DIM] = jnp.where(i >= k, jnp.exp(gaps), 0.0)

    for j in range(N_IN + 1):
        if j < N_IN:
            pass_near(j)
        for r in range(2 * HEADS):
            if r * (N_IN + 1) // (2 * HEADS) == j:
                decay_tables(r)
        if j == N_IN:
            for k in range(EARLY):
                pass_opposite(k)
        if j > 0:
            multiply_near(j - 1)

    def decay_size():
        return remote(
            dec.at[pl.ds(0, n_in - 1)], dec.at[pl.ds(0, n_in - 1)],
            dec_send, dec_recv, {"tensor": sib},
        )

    decay_size().wait_recv()
    my_head = place * chunk_rows // HEAD_DIM
    for i in range(n_in):
        edec[i : i + 1, :] = jnp.exp(dec[i, pl.ds(my_head, 1), :])

    for j in range(EARLY, N_IN + EARLY):
        if j < N_IN:
            pass_opposite(j)
        multiply_opposite(j - EARLY)
    remote(
        wo_ref, w2.at[pl.ds(HEADS * HEAD_DIM, HEADS * HEAD_DIM)],
        wo_send, wo_recv, {"tensor": sib},
    ).start()

    for h in range(HEADS):
        lanes = slice(h * HEAD_DIM, (h + 1) * HEAD_DIM)
        states = []
        for n in range(2):
            rows = slice(n * BLOCK, (n + 1) * BLOCK)
            keys = silu(block_of(1, n, lanes)).astype(BF16)
            values = block_of(2, n, lanes).astype(BF16)
            k_s[h, rows] = keys
            v_s[h, rows] = values
            weighted = (keys.astype(F32) * ek_s[n * HEADS + h]).astype(BF16)
            states.append(
                lax.dot_general(
                    weighted, values, (((0,), (0,)), ((), ())), preferred_element_type=F32
                )
            )
        u_s[h] = states[0]
        total = elast_s[HEADS + h : HEADS + h + 1, :] * states[0] + states[1]
        pieces = HEAD_DIM // chunk_rows
        st1[h * pieces : (h + 1) * pieces] = total.astype(BF16).reshape(
            pieces, chunk_rows, HEAD_DIM
        )

    for to in peers:
        remote(
            st1.at[to], rc1.at[place], p1_send, p1_recv, {"context": first + to}
        ).start()
    rc1[pl.ds(place, 1)] = st1[pl.ds(place, 1)]

    for j in range(N_IN):
        multiply(j, (OPPOSITE, 1), (0,))

    def attend(n):
        for h in range(HEADS):
            lanes = slice(h * HEAD_DIM, (h + 1) * HEAD_DIM)
            rows = slice(n * BLOCK, (n + 1) * BLOCK)
            queries = silu(block_of(0, n, lanes)).astype(BF16)
            weights = lax.dot_general(
                queries, k_s[h, rows, :], (((1,), (1,)), ((), ())), preferred_element_type=F32
            )
            weights = (weights * mask_s[n * HEADS + h]).astype(BF16)
            inner_s[h, 2 * n : 2 * n + 2] = jnp.dot(
                weights, v_s[h, rows, :], preferred_element_type=F32
            ).reshape(2, 2, ROWS, HEAD_DIM)
            scaled = queries.astype(F32).reshape(2, 2, ROWS, HEAD_DIM) * eq_s[n * HEADS + h]
            qs_s[h, 2 * n : 2 * n + 2] = scaled.astype(BF16)

    attend(0)

    def state_size(buffer, send, recv):
        others_of = buffer.at[pl.ds(0, n_in - 1)]
        return remote(others_of, others_of, send, recv, {"tensor": sib})

    state_size(rc1, p1_send, p1_recv).wait_recv()
    def group_copy(to):
        return remote(
            after, before.at[group], group_send.at[to], group_recv.at[group],
            {"context": to * n_in + place},
        )

    running = jnp.zeros((chunk_rows, HEAD_DIM), F32)
    kept = jnp.ones((16, HEAD_DIM), F32)
    for i in range(n_in):
        running = running * edec[i : i + 1, :] + rc1[i].astype(F32)
        kept = kept * edec[i : i + 1, :]
    after[0:chunk_rows] = running.astype(BF16)
    after[chunk_rows:] = two_parts(kept)
    for later_group in range(1, GROUPS):
        @pl.when(later_group > group)
        def _():
            pl.semaphore_wait(ready.at[later_group], 1)
            group_copy(later_group).start()

    running = jnp.zeros((chunk_rows, HEAD_DIM), F32)
    for earlier in range(GROUPS - 1):
        @pl.when(earlier < group)
        def _():
            remote(
                before.at[earlier], before.at[earlier], group_send.at[0],
                group_recv.at[earlier], {"tensor": sib},
            ).wait_recv()

        parts = before[earlier, chunk_rows:].astype(F32)
        running = running * (parts[0:1] + parts[8:9]) + before[earlier, 0:chunk_rows].astype(F32)
    for i in range(n_in):
        st2[i] = running.astype(BF16)
        running = running * edec[i : i + 1, :] + rc1[i].astype(F32)
    for to in peers:
        remote(
            st2.at[to], rc2.at[place], p2_send, p2_recv, {"context": first + to}
        ).start()
    rc2[pl.ds(place, 1)] = st2[pl.ds(place, 1)]

    attend(1)

    state_size(rc2, p2_send, p2_recv).wait_recv()

    pieces = HEAD_DIM // chunk_rows

    def normalize(which, target):
        for h in range(HEADS):
            lanes = slice(h * HEAD_DIM, (h + 1) * HEAD_DIM)
            entering = rc2[h * pieces : (h + 1) * pieces].reshape(HEAD_DIM, HEAD_DIM)
            later = elast_s[h : h + 1, :] * entering.astype(F32) + u_s[h]
            for n, state in enumerate((entering, later.astype(BF16))):
                queries = qs_s[h, 2 * n : 2 * n + 2, which].reshape(2 * ROWS, HEAD_DIM)
                attended = inner_s[h, 2 * n : 2 * n + 2, which].reshape(
                    2 * ROWS, HEAD_DIM
                ) + jnp.dot(queries, state, preferred_element_type=F32)
                size = jnp.mean(attended * attended, axis=1, keepdims=True)
                normed = (attended * lax.rsqrt(size + 1e-06)).astype(BF16)
                target[2 * n : 2 * n + 2, :, lanes] = normed.reshape(2, ROWS, HEAD_DIM)

    width = HEADS * HEAD_DIM
    normalize(other, nsend)
    norm_copy = remote(
        nsend, nrm.at[:, :, pl.ds(width, width)], n_send, n_recv, {"tensor": sib}
    )
    norm_copy.start()
    normalize(core, nrm)
    wo_copy.wait()
    w2_half = w2.at[pl.ds(width, width)]
    wo_wait = remote(w2_half, w2_half, wo_send, wo_recv, {"tensor": sib})
    wo_wait.wait_recv()
    norm_copy.wait_recv()

    def project(j):
        cols = out_cols(j)
        rows = nrm[...].reshape(N_Y * ROWS, 2 * width)
        chunk = jnp.dot(rows, w2[:, cols], preferred_element_type=F32).astype(BF16)
        part[:, :, cols] = chunk.reshape(N_Y, ROWS, nc)
        fwd, bwd = ring(j)
        remote(
            part.at[(y + 2) % N_Y, :, cols], relay.at[:, cols],
            rs_send, rs_relay.at[j], {"tensor": fwd * 2 + core},
        ).start()
        remote(
            part.at[bwd, :, cols], from_f.at[:, cols],
            rs_send, rs_f.at[j], {"tensor": bwd * 2 + core},
        ).start()

    def pass_on(j):
        cols = out_cols(j)
        fwd, _ = ring(j)
        remote(
            relay.at[:, cols], relay.at[:, cols], rs_send, rs_relay.at[j], {"tensor": sib}
        ).wait_recv()
        summed[:, cols] = (
            part[pl.ds(fwd, 1), :, cols].reshape(ROWS, nc).astype(F32)
            + relay[:, cols].astype(F32)
        ).astype(BF16)
        remote(
            summed.at[:, cols], from_b.at[:, cols],
            rs_sum_send, rs_b.at[j], {"tensor": fwd * 2 + core},
        ).start()

    def finish_rows(j):
        cols = out_cols(j)
        remote(
            from_f.at[:, cols], from_f.at[:, cols], rs_send, rs_f.at[j], {"tensor": sib}
        ).wait_recv()
        remote(
            from_b.at[:, cols], from_b.at[:, cols], rs_send, rs_b.at[j], {"tensor": sib}
        ).wait_recv()
        out_ref[:, cols] = (
            part[pl.ds(y, 1), :, cols].reshape(ROWS, nc).astype(F32)
            + from_f[:, cols].astype(F32)
            + from_b[:, cols].astype(F32)
        ).astype(out_ref.dtype)

    def project_step(j, carry):
        project(j)

        @pl.when(j >= LAG)
        def _():
            pass_on(j - LAG)

        return carry

    lax.fori_loop(0, OUT_CHUNKS, project_step, 0)

    def pass_step(j, carry):
        pass_on(j)
        finish_rows(j - (OUT_CHUNKS - LAG))
        return carry

    lax.fori_loop(OUT_CHUNKS - LAG, OUT_CHUNKS, pass_step, 0)

    seven = w2.at[pl.ds(0, 7 * ROWS)]
    remote(seven, seven, ag_send, ag_s.at[0], {"tensor": sib}).wait_send()
    wo_wait.wait_send()
    decay_size().wait_send()
    state_size(st1, p1_send, p1_recv).wait_send()
    state_size(st2, p2_send, p2_recv).wait_send()
    norm_copy.wait_send()

    for later_group in range(1, GROUPS):
        @pl.when(later_group > group)
        def _():
            group_copy(later_group).wait_send()


    def finish_step(j, carry):
        finish_rows(j)
        return carry

    lax.fori_loop(LAG, OUT_CHUNKS, finish_step, 0)
    two = part.at[pl.ds(0, 2)]
    remote(two, two, rs_send, rs_f.at[0], {"tensor": sib}).wait_send()
    remote(summed, summed, rs_sum_send, rs_b.at[0], {"tensor": sib}).wait_send()


def body(n_ctx, activations, w_qkv, w_out, log_decay):
    rows, d_model = activations.shape
    width = HEADS * HEAD_DIM
    n_in, chunk_rows = split(n_ctx)
    hbm = pl.BlockSpec(memory_space=pltpu.HBM)
    vmem = pl.BlockSpec(memory_space=pltpu.VMEM)
    dma = pltpu.SemaphoreType.DMA
    shard = N_TENSOR * rows
    scratch = [
        pltpu.VMEM((N_Y, 2, rows, d_model), BF16),
        pltpu.VMEM((3, d_model, width), BF16),
        pltpu.VMEM((2 * width, d_model), BF16),
        pltpu.VMEM((3, shard, width), F32),
        pltpu.VMEM((HEADS, N_Y, 2, rows, HEAD_DIM), BF16),
        pltpu.VMEM((HEADS, shard, HEAD_DIM), BF16),
        pltpu.VMEM((HEADS, shard, HEAD_DIM), BF16),
        pltpu.VMEM((2 * HEADS, BLOCK, BLOCK), F32),
        pltpu.VMEM((2 * HEADS, 2, 2, rows, HEAD_DIM), F32),
        pltpu.VMEM((2 * HEADS, BLOCK, HEAD_DIM), F32),
        pltpu.VMEM((HEADS, N_Y, 2, rows, HEAD_DIM), F32),
        pltpu.VMEM((HEADS, HEAD_DIM, HEAD_DIM), F32),
        pltpu.VMEM((HEADS, 2 * BLOCK), F32),
        pltpu.VMEM((2 * HEADS, BLOCK), F32),
        pltpu.VMEM((2 * HEADS, BLOCK), F32),
        pltpu.VMEM((2 * HEADS, HEAD_DIM), F32),
        pltpu.VMEM((2 * HEADS, HEAD_DIM), F32),
        pltpu.VMEM((n_in, 2 * HEADS, HEAD_DIM), F32),
        pltpu.VMEM((n_in, HEAD_DIM), F32),
        pltpu.VMEM((n_in, chunk_rows, HEAD_DIM), BF16),
        pltpu.VMEM((n_in, chunk_rows, HEAD_DIM), BF16),
        pltpu.VMEM((n_in, chunk_rows, HEAD_DIM), BF16),
        pltpu.VMEM((n_in, chunk_rows, HEAD_DIM), BF16),
        pltpu.VMEM((GROUPS - 1, chunk_rows + 16, HEAD_DIM), BF16),
        pltpu.VMEM((chunk_rows + 16, HEAD_DIM), BF16),
        pltpu.VMEM((N_Y, rows, width), BF16),
        pltpu.VMEM((N_Y, rows, 2 * width), BF16),
        pltpu.VMEM((N_Y, rows, d_model), BF16),
        pltpu.VMEM((rows, d_model), BF16),
        pltpu.VMEM((rows, d_model), BF16),
        pltpu.VMEM((rows, d_model), BF16),
        pltpu.VMEM((rows, d_model), BF16),
        dma,
        dma((N_IN,)),
        dma((N_IN,)),
        dma((N_IN,)),
        dma((N_IN,)),
        dma((N_IN,)),
        dma((N_IN,)),
        dma((N_IN,)),
        dma,
        dma,
        dma,
        dma,
        dma,
        dma,
        dma,
        dma,
        dma,
        dma,
        dma,
        dma,
        dma((OUT_CHUNKS,)),
        dma((OUT_CHUNKS,)),
        dma((OUT_CHUNKS,)),
        dma,
        dma,
        dma((GROUPS,)),
        dma((GROUPS,)),
        pltpu.SemaphoreType.REGULAR((GROUPS,)),
    ]
    return pl.pallas_call(
        functools.partial(kernel, n_ctx),
        out_shape=jax.ShapeDtypeStruct((rows, d_model), BF16),
        in_specs=[hbm, hbm, hbm, hbm],
        out_specs=vmem,
        scratch_shapes=scratch,
        compiler_params=pltpu.CompilerParams(
            collective_id=0, has_side_effects=True, vmem_limit_bytes=52 * 1024 * 1024
        ),
    )(*(
        pltpu.with_memory_space_constraint(array, pltpu.HBM)
        for array in (activations, w_qkv.transpose(1, 0, 2), w_out, log_decay)
    ))


def solution(mesh):
    in_specs = (
        P(("context", "tensor"), None),
        P(None, None, "tensor"),
        P("tensor", None),
        P("tensor", "context"),
    )
    out_specs = P(("context", "tensor"), None)
    return jax.shard_map(
        functools.partial(body, mesh.shape["context"]),
        mesh=mesh, in_specs=in_specs, out_specs=out_specs, check_vma=False,
    )
```

```python
import functools

import jax
import jax.numpy as jnp
from jax import lax
from jax.experimental import pallas as pl
from jax.experimental.pallas import tpu as pltpu
from jax.sharding import PartitionSpec as P

HEAD_DIM = 128
BLOCK = 256
ROWS = 64
HEADS = 4
N_TENSOR = 8
N_X = 4
N_Y = 4
GROUPS = 4
IN_CHUNKS = (512, 512, 512, 512, 512, 256, 256)
N_IN = len(IN_CHUNKS)
OUT_CHUNKS = 6
LAG = 3
EARLY = 2
OWN, UP, DOWN, OPPOSITE = range(N_Y)
F32 = jnp.float32
BF16 = jnp.bfloat16


def silu(v):
    half = 0.5 * v
    return half + half * jnp.tanh(half)


def split(n_ctx):
    n_in = n_ctx // GROUPS
    return n_in, HEADS * HEAD_DIM // n_in


def kernel(
    n_ctx, x_ref, w_ref, wo_ref, ld_ref, out_ref,
    xall, wv, w2, acc, qs_s, k_s, v_s, mask_s, eq_s, ek_s, inner_s, u_s,
    ld4, ld8, cum_s, elast_s, dsend, dec, edec,
    st1, rc1, st2, rc2, before, after, nsend, nrm, part, relay, summed, from_b, from_f,
    ag_send, ag_up, ag_down, ag_o, ag_s, ag_so, own_sem, w_sem, wo_own, wo_send, wo_recv,
    dec_send, dec_recv, p1_send, p1_recv, p2_send, p2_recv, n_send, n_recv,
    rs_send, rs_relay, rs_b, rs_f, rs_sum_send, ld_sem, group_send, group_recv, ready,
):
    ctx = lax.axis_index("context")
    t = lax.axis_index("tensor")
    y = t // 2
    core = t % 2
    other = 1 - core
    sib = y * 2 + other
    d_model = x_ref.shape[1]
    nc = d_model // OUT_CHUNKS

    n_in, chunk_rows = split(n_ctx)
    group, place = ctx // n_in, ctx % n_in
    first = group * n_in

    others = sorted(
        ((dz, dx) for dz in range(n_in // N_X) for dx in range(N_X) if dz or dx),
        key=lambda d: -(d[0] + min(d[1], N_X - d[1])),
    )
    peers = [
        (place // N_X + dz) % (n_in // N_X) * N_X + (place % N_X + dx) % N_X
        for dz, dx in others
    ]

    def remote(src, dst, send, recv, device):
        return pltpu.make_async_remote_copy(
            src_ref=src, dst_ref=dst, send_sem=send, recv_sem=recv,
            device_id=device, device_id_type=pl.DeviceIdType.MESH,
        )

    def ring(j):
        step = 1 - 2 * ((j + core) % 2)
        fwd = (y + step + N_Y) % N_Y
        bwd = (y - step + N_Y) % N_Y
        return fwd, bwd

    def in_cols(j):
        return pl.ds(sum(IN_CHUNKS[:j]), IN_CHUNKS[j])

    def out_cols(j):
        return pl.ds(pl.multiple_of(j * nc, nc), nc)

    def w_copy(j):
        rows = in_cols(j)
        return pltpu.make_async_copy(w_ref.at[:, rows, :], wv.at[:, rows, :], w_sem.at[j])

    def own_copy(j):
        cols = in_cols(j)
        return pltpu.make_async_copy(x_ref.at[:, cols], xall.at[OWN, core, :, cols], own_sem.at[j])

    up, down = (y + 1) % N_Y * 2, (y + N_Y - 1) % N_Y * 2

    def send_own(j):
        cols = in_cols(j)
        src = xall.at[OWN, core, :, cols]
        own_copy(j).wait()
        remote(
            src, xall.at[DOWN, core, :, cols], ag_send, ag_down.at[j], {"tensor": up + core}
        ).start()
        remote(
            src, xall.at[UP, core, :, cols], ag_send, ag_up.at[j], {"tensor": down + core}
        ).start()
        remote(src, src, ag_send, ag_s.at[j], {"tensor": sib}).start()

    def arrived(ref, sem):
        remote(ref, ref, ag_send, sem, {"tensor": sib}).wait_recv()

    def pass_near(j):
        cols = in_cols(j)
        arrived(xall.at[DOWN, core, :, cols], ag_down.at[j])
        arrived(xall.at[UP, core, :, cols], ag_up.at[j])
        upward = (j + core) % 2
        chip = (y + 2 * upward + N_Y - 1) % N_Y * 2
        src = xall.at[UP + upward, core, :, cols]
        dst = xall.at[OPPOSITE, core, :, cols]
        remote(src, dst, ag_send, ag_o.at[j], {"tensor": chip + core}).start()
        if j == N_IN - 1:
            remote(src, dst, ag_send, ag_so.at[j], {"tensor": chip + other}).start()
        near = xall.at[pl.ds(UP, 2), core, :, cols]
        remote(near, near, ag_send, ag_s.at[j], {"tensor": sib}).start()

    def pass_opposite(j):
        ref = xall.at[OPPOSITE, core, :, in_cols(j)]
        arrived(ref, ag_o.at[j])
        if j < N_IN - 1:
            remote(ref, ref, ag_send, ag_so.at[j], {"tensor": sib}).start()

    def multiply(j, slots, parts):
        first, count = slots
        rows = slice(first * 2 * ROWS, (first + count) * 2 * ROWS)
        values = xall[first : first + count, :, :, in_cols(j)].reshape(
            count * 2 * ROWS, IN_CHUNKS[j]
        )
        for i in parts:
            product = jnp.dot(values, wv[i, in_cols(j), :], preferred_element_type=F32)
            acc[i, rows] = product if j == 0 else acc[i, rows] + product

    def multiply_near(j):
        w_copy(j).wait()
        arrived(xall.at[pl.ds(OWN, 3), other, :, in_cols(j)], ag_s.at[j])
        multiply(j, (OWN, 3), (0, 1, 2))

    def multiply_opposite(j):
        arrived(xall.at[OPPOSITE, other, :, in_cols(j)], ag_so.at[j])
        multiply(j, (OPPOSITE, 1), (1, 2))

    def rows_of(i, chip, lanes):
        ahead = (chip - y + N_Y) % N_Y
        slot = ahead + ahead // 2 * (5 - 2 * ahead)
        return acc[i, pl.ds(pl.multiple_of(slot * 2 * ROWS, 2 * ROWS), 2 * ROWS), lanes]

    def block_of(i, n, lanes):
        return jnp.concatenate([rows_of(i, 2 * n, lanes), rows_of(i, 2 * n + 1, lanes)], axis=0)

    def two_parts(value):
        high = value.astype(BF16).astype(F32)
        row = lax.broadcasted_iota(jnp.int32, (16, HEAD_DIM), 0)
        return jnp.where(row < 8, high, value - high).astype(BF16)

    ld_copy = pltpu.make_async_copy(ld_ref, ld4, ld_sem)
    ld_copy.start()
    for j in range(N_IN):
        own_copy(j).start()
        w_copy(j).start()
    wo_copy = pltpu.make_async_copy(wo_ref, w2.at[pl.ds(0, HEADS * HEAD_DIM)], wo_own)
    wo_copy.start()

    barrier = pltpu.get_barrier_semaphore()
    for peer in (up + core, down + core, sib, up + other, down + other):
        pl.semaphore_signal(
            barrier, inc=1, device_id={"tensor": peer}, device_id_type=pl.DeviceIdType.MESH
        )

    for to in peers:
        pl.semaphore_signal(
            barrier, inc=1, device_id={"context": first + to},
            device_id_type=pl.DeviceIdType.MESH,
        )

    for later_group in range(1, GROUPS):
        @pl.when(later_group > group)
        def _():
            pl.semaphore_signal(
                barrier, inc=1, device_id={"context": later_group * n_in + place},
                device_id_type=pl.DeviceIdType.MESH,
            )

    pl.semaphore_wait(barrier, 5 + n_in - 1 + group)

    for j in range(N_IN):
        send_own(j)

    for earlier in range(GROUPS - 1):
        @pl.when(earlier < group)
        def _():
            pl.semaphore_signal(
                ready.at[group], inc=1, device_id={"context": earlier * n_in + place},
                device_id_type=pl.DeviceIdType.MESH,
            )

        @pl.when(earlier >= group)
        def _():
            before[earlier, 0:chunk_rows] = jnp.zeros((chunk_rows, HEAD_DIM), BF16)
            before[earlier, chunk_rows:] = two_parts(jnp.ones((16, HEAD_DIM), F32))

    ld_copy.wait()
    ld8[0:HEADS, :] = ld4[:, 0:BLOCK]
    ld8[HEADS : 2 * HEADS, :] = ld4[:, BLOCK : 2 * BLOCK]
    cum = ld8[...]
    lane = lax.broadcasted_iota(jnp.int32, (2 * HEADS, BLOCK), 1)
    shift = 1
    while shift < BLOCK:
        cum = cum + jnp.where(lane >= shift, pltpu.roll(cum, shift, 1), 0.0)
        shift *= 2
    cum_s[...] = cum
    last = jnp.broadcast_to(cum[:, BLOCK - 1 : BLOCK], (2 * HEADS, HEAD_DIM))
    elast_s[...] = jnp.exp(last)
    both = last + pltpu.roll(last, HEADS, 0)
    dsend[...] = both
    dec[pl.ds(place, 1)] = both[None]

    for to in peers:
        remote(dsend, dec.at[place], dec_send, dec_recv, {"context": first + to}).start()

    def decay_tables(r):
        row = cum_s[pl.ds(r, 1), :]
        column = jnp.transpose(jnp.broadcast_to(row, (HEAD_DIM, BLOCK)))
        end = row[:, BLOCK - 1 : BLOCK]
        eq_s[r] = jnp.exp(column).reshape(2, 2, ROWS, HEAD_DIM)
        ek_s[r] = jnp.exp(end - column)
        for half in range(2):
            at = half * HEAD_DIM
            gaps = jnp.minimum(column - row[:, at : at + HEAD_DIM], 0.0)
            i = lax.broadcasted_iota(jnp.int32, (BLOCK, HEAD_DIM), 0)
            k = lax.broadcasted_iota(jnp.int32, (BLOCK, HEAD_DIM), 1) + at
            mask_s[r, :, at : at + HEAD_DIM] = jnp.where(i >= k, jnp.exp(gaps), 0.0)

    for j in range(N_IN + 1):
        if j < N_IN:
            pass_near(j)
        for r in range(2 * HEADS):
            if r * (N_IN + 1) // (2 * HEADS) == j:
                decay_tables(r)
        if j == N_IN:
            for k in range(EARLY):
                pass_opposite(k)
        if j > 0:
            multiply_near(j - 1)

    def decay_size():
        return remote(
            dec.at[pl.ds(0, n_in - 1)], dec.at[pl.ds(0, n_in - 1)],
            dec_send, dec_recv, {"tensor": sib},
        )

    decay_size().wait_recv()
    my_head = place * chunk_rows // HEAD_DIM
    for i in range(n_in):
        edec[i : i + 1, :] = jnp.exp(dec[i, pl.ds(my_head, 1), :])

    for j in range(EARLY, N_IN + EARLY):
        if j < N_IN:
            pass_opposite(j)
        multiply_opposite(j - EARLY)
    remote(
        wo_ref, w2.at[pl.ds(HEADS * HEAD_DIM, HEADS * HEAD_DIM)],
        wo_send, wo_recv, {"tensor": sib},
    ).start()

    for h in range(HEADS):
        lanes = slice(h * HEAD_DIM, (h + 1) * HEAD_DIM)
        states = []
        for n in range(2):
            rows = slice(n * BLOCK, (n + 1) * BLOCK)
            keys = silu(block_of(1, n, lanes)).astype(BF16)
            values = block_of(2, n, lanes).astype(BF16)
            k_s[h, rows] = keys
            v_s[h, rows] = values
            weighted = (keys.astype(F32) * ek_s[n * HEADS + h]).astype(BF16)
            states.append(
                lax.dot_general(
                    weighted, values, (((0,), (0,)), ((), ())), preferred_element_type=F32
                )
            )
        u_s[h] = states[0]
        total = elast_s[HEADS + h : HEADS + h + 1, :] * states[0] + states[1]
        pieces = HEAD_DIM // chunk_rows
        st1[h * pieces : (h + 1) * pieces] = total.astype(BF16).reshape(
            pieces, chunk_rows, HEAD_DIM
        )

    for to in peers:
        remote(
            st1.at[to], rc1.at[place], p1_send, p1_recv, {"context": first + to}
        ).start()
    rc1[pl.ds(place, 1)] = st1[pl.ds(place, 1)]

    for j in range(N_IN):
        multiply(j, (OPPOSITE, 1), (0,))

    def attend(n):
        for h in range(HEADS):
            lanes = slice(h * HEAD_DIM, (h + 1) * HEAD_DIM)
            rows = slice(n * BLOCK, (n + 1) * BLOCK)
            queries = silu(block_of(0, n, lanes)).astype(BF16)
            weights = lax.dot_general(
                queries, k_s[h, rows, :], (((1,), (1,)), ((), ())), preferred_element_type=F32
            )
            weights = (weights * mask_s[n * HEADS + h]).astype(BF16)
            inner_s[h, 2 * n : 2 * n + 2] = jnp.dot(
                weights, v_s[h, rows, :], preferred_element_type=F32
            ).reshape(2, 2, ROWS, HEAD_DIM)
            scaled = queries.astype(F32).reshape(2, 2, ROWS, HEAD_DIM) * eq_s[n * HEADS + h]
            qs_s[h, 2 * n : 2 * n + 2] = scaled.astype(BF16)

    attend(0)

    def state_size(buffer, send, recv):
        others_of = buffer.at[pl.ds(0, n_in - 1)]
        return remote(others_of, others_of, send, recv, {"tensor": sib})

    state_size(rc1, p1_send, p1_recv).wait_recv()
    def group_copy(to):
        return remote(
            after, before.at[group], group_send.at[to], group_recv.at[group],
            {"context": to * n_in + place},
        )

    running = jnp.zeros((chunk_rows, HEAD_DIM), F32)
    kept = jnp.ones((16, HEAD_DIM), F32)
    for i in range(n_in):
        running = running * edec[i : i + 1, :] + rc1[i].astype(F32)
        kept = kept * edec[i : i + 1, :]
    after[0:chunk_rows] = running.astype(BF16)
    after[chunk_rows:] = two_parts(kept)
    for later_group in range(1, GROUPS):
        @pl.when(later_group > group)
        def _():
            pl.semaphore_wait(ready.at[later_group], 1)
            group_copy(later_group).start()

    running = jnp.zeros((chunk_rows, HEAD_DIM), F32)
    for earlier in range(GROUPS - 1):
        @pl.when(earlier < group)
        def _():
            remote(
                before.at[earlier], before.at[earlier], group_send.at[0],
                group_recv.at[earlier], {"tensor": sib},
            ).wait_recv()

        parts = before[earlier, chunk_rows:].astype(F32)
        running = running * (parts[0:1] + parts[8:9]) + before[earlier, 0:chunk_rows].astype(F32)
    for i in range(n_in):
        st2[i] = running.astype(BF16)
        running = running * edec[i : i + 1, :] + rc1[i].astype(F32)
    for to in peers:
        remote(
            st2.at[to], rc2.at[place], p2_send, p2_recv, {"context": first + to}
        ).start()
    rc2[pl.ds(place, 1)] = st2[pl.ds(place, 1)]

    attend(1)

    state_size(rc2, p2_send, p2_recv).wait_recv()

    pieces = HEAD_DIM // chunk_rows

    def normalize(which, target):
        for h in range(HEADS):
            lanes = slice(h * HEAD_DIM, (h + 1) * HEAD_DIM)
            entering = rc2[h * pieces : (h + 1) * pieces].reshape(HEAD_DIM, HEAD_DIM)
            later = elast_s[h : h + 1, :] * entering.astype(F32) + u_s[h]
            for n, state in enumerate((entering, later.astype(BF16))):
                queries = qs_s[h, 2 * n : 2 * n + 2, which].reshape(2 * ROWS, HEAD_DIM)
                attended = inner_s[h, 2 * n : 2 * n + 2, which].reshape(
                    2 * ROWS, HEAD_DIM
                ) + jnp.dot(queries, state, preferred_element_type=F32)
                size = jnp.mean(attended * attended, axis=1, keepdims=True)
                normed = (attended * lax.rsqrt(size + 1e-06)).astype(BF16)
                target[2 * n : 2 * n + 2, :, lanes] = normed.reshape(2, ROWS, HEAD_DIM)

    width = HEADS * HEAD_DIM
    normalize(other, nsend)
    norm_copy = remote(
        nsend, nrm.at[:, :, pl.ds(width, width)], n_send, n_recv, {"tensor": sib}
    )
    norm_copy.start()
    normalize(core, nrm)
    wo_copy.wait()
    w2_half = w2.at[pl.ds(width, width)]
    wo_wait = remote(w2_half, w2_half, wo_send, wo_recv, {"tensor": sib})
    wo_wait.wait_recv()
    norm_copy.wait_recv()

    def project(j):
        cols = out_cols(j)
        rows = nrm[...].reshape(N_Y * ROWS, 2 * width)
        chunk = jnp.dot(rows, w2[:, cols], preferred_element_type=F32).astype(BF16)
        part[:, :, cols] = chunk.reshape(N_Y, ROWS, nc)
        fwd, bwd = ring(j)
        remote(
            part.at[(y + 2) % N_Y, :, cols], relay.at[:, cols],
            rs_send, rs_relay.at[j], {"tensor": fwd * 2 + core},
        ).start()
        remote(
            part.at[bwd, :, cols], from_f.at[:, cols],
            rs_send, rs_f.at[j], {"tensor": bwd * 2 + core},
        ).start()

    def pass_on(j):
        cols = out_cols(j)
        fwd, _ = ring(j)
        remote(
            relay.at[:, cols], relay.at[:, cols], rs_send, rs_relay.at[j], {"tensor": sib}
        ).wait_recv()
        summed[:, cols] = (
            part[pl.ds(fwd, 1), :, cols].reshape(ROWS, nc).astype(F32)
            + relay[:, cols].astype(F32)
        ).astype(BF16)
        remote(
            summed.at[:, cols], from_b.at[:, cols],
            rs_sum_send, rs_b.at[j], {"tensor": fwd * 2 + core},
        ).start()

    def finish_rows(j):
        cols = out_cols(j)
        remote(
            from_f.at[:, cols], from_f.at[:, cols], rs_send, rs_f.at[j], {"tensor": sib}
        ).wait_recv()
        remote(
            from_b.at[:, cols], from_b.at[:, cols], rs_send, rs_b.at[j], {"tensor": sib}
        ).wait_recv()
        out_ref[:, cols] = (
            part[pl.ds(y, 1), :, cols].reshape(ROWS, nc).astype(F32)
            + from_f[:, cols].astype(F32)
            + from_b[:, cols].astype(F32)
        ).astype(out_ref.dtype)

    def project_step(j, carry):
        project(j)

        @pl.when(j >= LAG)
        def _():
            pass_on(j - LAG)

        return carry

    lax.fori_loop(0, OUT_CHUNKS, project_step, 0)

    def pass_step(j, carry):
        pass_on(j)
        finish_rows(j - (OUT_CHUNKS - LAG))
        return carry

    lax.fori_loop(OUT_CHUNKS - LAG, OUT_CHUNKS, pass_step, 0)

    seven = w2.at[pl.ds(0, 7 * ROWS)]
    remote(seven, seven, ag_send, ag_s.at[0], {"tensor": sib}).wait_send()
    wo_wait.wait_send()
    decay_size().wait_send()
    state_size(st1, p1_send, p1_recv).wait_send()
    state_size(st2, p2_send, p2_recv).wait_send()
    norm_copy.wait_send()

    for later_group in range(1, GROUPS):
        @pl.when(later_group > group)
        def _():
            group_copy(later_group).wait_send()


    def finish_step(j, carry):
        finish_rows(j)
        return carry

    lax.fori_loop(LAG, OUT_CHUNKS, finish_step, 0)
    two = part.at[pl.ds(0, 2)]
    remote(two, two, rs_send, rs_f.at[0], {"tensor": sib}).wait_send()
    remote(summed, summed, rs_sum_send, rs_b.at[0], {"tensor": sib}).wait_send()


def body(n_ctx, activations, w_qkv, w_out, log_decay):
    rows, d_model = activations.shape
    width = HEADS * HEAD_DIM
    n_in, chunk_rows = split(n_ctx)
    hbm = pl.BlockSpec(memory_space=pltpu.HBM)
    vmem = pl.BlockSpec(memory_space=pltpu.VMEM)
    dma = pltpu.SemaphoreType.DMA
    shard = N_TENSOR * rows
    scratch = [
        pltpu.VMEM((N_Y, 2, rows, d_model), BF16),
        pltpu.VMEM((3, d_model, width), BF16),
        pltpu.VMEM((2 * width, d_model), BF16),
        pltpu.VMEM((3, shard, width), F32),
        pltpu.VMEM((HEADS, N_Y, 2, rows, HEAD_DIM), BF16),
        pltpu.VMEM((HEADS, shard, HEAD_DIM), BF16),
        pltpu.VMEM((HEADS, shard, HEAD_DIM), BF16),
        pltpu.VMEM((2 * HEADS, BLOCK, BLOCK), F32),
        pltpu.VMEM((2 * HEADS, 2, 2, rows, HEAD_DIM), F32),
        pltpu.VMEM((2 * HEADS, BLOCK, HEAD_DIM), F32),
        pltpu.VMEM((HEADS, N_Y, 2, rows, HEAD_DIM), F32),
        pltpu.VMEM((HEADS, HEAD_DIM, HEAD_DIM), F32),
        pltpu.VMEM((HEADS, 2 * BLOCK), F32),
        pltpu.VMEM((2 * HEADS, BLOCK), F32),
        pltpu.VMEM((2 * HEADS, BLOCK), F32),
        pltpu.VMEM((2 * HEADS, HEAD_DIM), F32),
        pltpu.VMEM((2 * HEADS, HEAD_DIM), F32),
        pltpu.VMEM((n_in, 2 * HEADS, HEAD_DIM), F32),
        pltpu.VMEM((n_in, HEAD_DIM), F32),
        pltpu.VMEM((n_in, chunk_rows, HEAD_DIM), BF16),
        pltpu.VMEM((n_in, chunk_rows, HEAD_DIM), BF16),
        pltpu.VMEM((n_in, chunk_rows, HEAD_DIM), BF16),
        pltpu.VMEM((n_in, chunk_rows, HEAD_DIM), BF16),
        pltpu.VMEM((GROUPS - 1, chunk_rows + 16, HEAD_DIM), BF16),
        pltpu.VMEM((chunk_rows + 16, HEAD_DIM), BF16),
        pltpu.VMEM((N_Y, rows, width), BF16),
        pltpu.VMEM((N_Y, rows, 2 * width), BF16),
        pltpu.VMEM((N_Y, rows, d_model), BF16),
        pltpu.VMEM((rows, d_model), BF16),
        pltpu.VMEM((rows, d_model), BF16),
        pltpu.VMEM((rows, d_model), BF16),
        pltpu.VMEM((rows, d_model), BF16),
        dma,
        dma((N_IN,)),
        dma((N_IN,)),
        dma((N_IN,)),
        dma((N_IN,)),
        dma((N_IN,)),
        dma((N_IN,)),
        dma((N_IN,)),
        dma,
        dma,
        dma,
        dma,
        dma,
        dma,
        dma,
        dma,
        dma,
        dma,
        dma,
        dma,
        dma((OUT_CHUNKS,)),
        dma((OUT_CHUNKS,)),
        dma((OUT_CHUNKS,)),
        dma,
        dma,
        dma((GROUPS,)),
        dma((GROUPS,)),
        pltpu.SemaphoreType.REGULAR((GROUPS,)),
    ]
    return pl.pallas_call(
        functools.partial(kernel, n_ctx),
        out_shape=jax.ShapeDtypeStruct((rows, d_model), BF16),
        in_specs=[hbm, hbm, hbm, hbm],
        out_specs=vmem,
        scratch_shapes=scratch,
        compiler_params=pltpu.CompilerParams(
            collective_id=0, has_side_effects=True, vmem_limit_bytes=52 * 1024 * 1024
        ),
    )(*(
        pltpu.with_memory_space_constraint(array, pltpu.HBM)
        for array in (activations, w_qkv.transpose(1, 0, 2), w_out, log_decay)
    ))


def solution(mesh):
    in_specs = (
        P(("context", "tensor"), None),
        P(None, None, "tensor"),
        P("tensor", None),
        P("tensor", "context"),
    )
    out_specs = P(("context", "tensor"), None)
    return jax.shard_map(
        functools.partial(body, mesh.shape["context"]),
        mesh=mesh, in_specs=in_specs, out_specs=out_specs, check_vma=False,
    )
```

```python
import functools

import jax
import jax.numpy as jnp
from jax import lax
from jax.experimental import pallas as pl
from jax.experimental.pallas import tpu as pltpu
from jax.sharding import PartitionSpec as P

HEAD_DIM = 128
BLOCK = 256
ROWS = 64
HEADS = 4
N_TENSOR = 8
N_X = 4
N_Y = 4
GROUPS = 4
IN_CHUNKS = (512, 512, 512, 512, 512, 256, 256)
N_IN = len(IN_CHUNKS)
OUT_CHUNKS = 6
LAG = 3
EARLY = 3
OWN, UP, DOWN, OPPOSITE = range(N_Y)
F32 = jnp.float32
BF16 = jnp.bfloat16


def silu(v):
    half = 0.5 * v
    return half + half * jnp.tanh(half)


def split(n_ctx):
    n_in = n_ctx // GROUPS
    return n_in, HEADS * HEAD_DIM // n_in


def kernel(
    n_ctx, x_ref, w_ref, wo_ref, ld_ref, out_ref,
    xall, wv, w2, acc, qs_s, k_s, v_s, mask_s, eq_s, ek_s, inner_s, u_s,
    ld4, ld8, cum_s, elast_s, dsend, dec, edec,
    st1, rc1, st2, rc2, before, after, nsend, nrm, part, relay, summed, from_b, from_f,
    ag_send, ag_up, ag_down, ag_o, ag_s, ag_so, own_sem, w_sem, wo_own, wo_send, wo_recv,
    dec_send, dec_recv, p1_send, p1_recv, p2_send, p2_recv, n_send, n_recv,
    rs_send, rs_relay, rs_b, rs_f, rs_sum_send, ld_sem, group_send, group_recv, ready,
):
    ctx = lax.axis_index("context")
    t = lax.axis_index("tensor")
    y = t // 2
    core = t % 2
    other = 1 - core
    sib = y * 2 + other
    d_model = x_ref.shape[1]
    nc = d_model // OUT_CHUNKS

    n_in, chunk_rows = split(n_ctx)
    group, place = ctx // n_in, ctx % n_in
    first = group * n_in

    others = sorted(
        ((dz, dx) for dz in range(n_in // N_X) for dx in range(N_X) if dz or dx),
        key=lambda d: -(d[0] + min(d[1], N_X - d[1])),
    )
    peers = [
        (place // N_X + dz) % (n_in // N_X) * N_X + (place % N_X + dx) % N_X
        for dz, dx in others
    ]

    def remote(src, dst, send, recv, device):
        return pltpu.make_async_remote_copy(
            src_ref=src, dst_ref=dst, send_sem=send, recv_sem=recv,
            device_id=device, device_id_type=pl.DeviceIdType.MESH,
        )

    def ring(j):
        step = 1 - 2 * ((j + core) % 2)
        fwd = (y + step + N_Y) % N_Y
        bwd = (y - step + N_Y) % N_Y
        return fwd, bwd

    def in_cols(j):
        return pl.ds(sum(IN_CHUNKS[:j]), IN_CHUNKS[j])

    def out_cols(j):
        return pl.ds(pl.multiple_of(j * nc, nc), nc)

    def w_copy(j):
        rows = in_cols(j)
        return pltpu.make_async_copy(w_ref.at[:, rows, :], wv.at[:, rows, :], w_sem.at[j])

    def own_copy(j):
        cols = in_cols(j)
        return pltpu.make_async_copy(x_ref.at[:, cols], xall.at[OWN, core, :, cols], own_sem.at[j])

    up, down = (y + 1) % N_Y * 2, (y + N_Y - 1) % N_Y * 2

    def send_own(j):
        cols = in_cols(j)
        src = xall.at[OWN, core, :, cols]
        own_copy(j).wait()
        remote(
            src, xall.at[DOWN, core, :, cols], ag_send, ag_down.at[j], {"tensor": up + core}
        ).start()
        remote(
            src, xall.at[UP, core, :, cols], ag_send, ag_up.at[j], {"tensor": down + core}
        ).start()
        remote(src, src, ag_send, ag_s.at[j], {"tensor": sib}).start()

    def arrived(ref, sem):
        remote(ref, ref, ag_send, sem, {"tensor": sib}).wait_recv()

    def pass_near(j):
        cols = in_cols(j)
        arrived(xall.at[DOWN, core, :, cols], ag_down.at[j])
        arrived(xall.at[UP, core, :, cols], ag_up.at[j])
        upward = (j + core) % 2
        chip = (y + 2 * upward + N_Y - 1) % N_Y * 2
        src = xall.at[UP + upward, core, :, cols]
        dst = xall.at[OPPOSITE, core, :, cols]
        remote(src, dst, ag_send, ag_o.at[j], {"tensor": chip + core}).start()
        if j >= N_IN - 2:
            remote(src, dst, ag_send, ag_so.at[j], {"tensor": chip + other}).start()
        near = xall.at[pl.ds(UP, 2), core, :, cols]
        remote(near, near, ag_send, ag_s.at[j], {"tensor": sib}).start()

    def pass_opposite(j):
        ref = xall.at[OPPOSITE, core, :, in_cols(j)]
        arrived(ref, ag_o.at[j])
        if j < N_IN - 2:
            remote(ref, ref, ag_send, ag_so.at[j], {"tensor": sib}).start()

    def multiply(j, slots, parts):
        first, count = slots
        rows = slice(first * 2 * ROWS, (first + count) * 2 * ROWS)
        values = xall[first : first + count, :, :, in_cols(j)].reshape(
            count * 2 * ROWS, IN_CHUNKS[j]
        )
        for i in parts:
            product = jnp.dot(values, wv[i, in_cols(j), :], preferred_element_type=F32)
            acc[i, rows] = product if j == 0 else acc[i, rows] + product

    def multiply_near(j):
        w_copy(j).wait()
        arrived(xall.at[pl.ds(OWN, 3), other, :, in_cols(j)], ag_s.at[j])
        multiply(j, (OWN, 3), (0, 1, 2))

    def multiply_opposite(j):
        arrived(xall.at[OPPOSITE, other, :, in_cols(j)], ag_so.at[j])
        multiply(j, (OPPOSITE, 1), (1, 2))

    def rows_of(i, chip, lanes):
        ahead = (chip - y + N_Y) % N_Y
        slot = ahead + ahead // 2 * (5 - 2 * ahead)
        return acc[i, pl.ds(pl.multiple_of(slot * 2 * ROWS, 2 * ROWS), 2 * ROWS), lanes]

    def block_of(i, n, lanes):
        return jnp.concatenate([rows_of(i, 2 * n, lanes), rows_of(i, 2 * n + 1, lanes)], axis=0)

    def two_parts(value):
        high = value.astype(BF16).astype(F32)
        row = lax.broadcasted_iota(jnp.int32, (16, HEAD_DIM), 0)
        return jnp.where(row < 8, high, value - high).astype(BF16)

    ld_copy = pltpu.make_async_copy(ld_ref, ld4, ld_sem)
    ld_copy.start()
    for j in range(N_IN):
        own_copy(j).start()
        w_copy(j).start()
    wo_copy = pltpu.make_async_copy(wo_ref, w2.at[pl.ds(0, HEADS * HEAD_DIM)], wo_own)
    wo_copy.start()

    barrier = pltpu.get_barrier_semaphore()
    for peer in (up + core, down + core, sib, up + other, down + other):
        pl.semaphore_signal(
            barrier, inc=1, device_id={"tensor": peer}, device_id_type=pl.DeviceIdType.MESH
        )

    for to in peers:
        pl.semaphore_signal(
            barrier, inc=1, device_id={"context": first + to},
            device_id_type=pl.DeviceIdType.MESH,
        )

    for later_group in range(1, GROUPS):
        @pl.when(later_group > group)
        def _():
            pl.semaphore_signal(
                barrier, inc=1, device_id={"context": later_group * n_in + place},
                device_id_type=pl.DeviceIdType.MESH,
            )

    pl.semaphore_wait(barrier, 5 + n_in - 1 + group)

    for j in range(N_IN):
        send_own(j)

    for earlier in range(GROUPS - 1):
        @pl.when(earlier < group)
        def _():
            pl.semaphore_signal(
                ready.at[group], inc=1, device_id={"context": earlier * n_in + place},
                device_id_type=pl.DeviceIdType.MESH,
            )

        @pl.when(earlier >= group)
        def _():
            before[earlier, 0:chunk_rows] = jnp.zeros((chunk_rows, HEAD_DIM), BF16)
            before[earlier, chunk_rows:] = two_parts(jnp.ones((16, HEAD_DIM), F32))

    ld_copy.wait()
    ld8[0:HEADS, :] = ld4[:, 0:BLOCK]
    ld8[HEADS : 2 * HEADS, :] = ld4[:, BLOCK : 2 * BLOCK]
    cum = ld8[...]
    lane = lax.broadcasted_iota(jnp.int32, (2 * HEADS, BLOCK), 1)
    shift = 1
    while shift < BLOCK:
        cum = cum + jnp.where(lane >= shift, pltpu.roll(cum, shift, 1), 0.0)
        shift *= 2
    cum_s[...] = cum
    last = jnp.broadcast_to(cum[:, BLOCK - 1 : BLOCK], (2 * HEADS, HEAD_DIM))
    elast_s[...] = jnp.exp(last)
    both = last + pltpu.roll(last, HEADS, 0)
    dsend[...] = both
    dec[pl.ds(place, 1)] = both[None]

    for to in peers:
        remote(dsend, dec.at[place], dec_send, dec_recv, {"context": first + to}).start()

    def decay_tables(r):
        row = cum_s[pl.ds(r, 1), :]
        column = jnp.transpose(jnp.broadcast_to(row, (HEAD_DIM, BLOCK)))
        end = row[:, BLOCK - 1 : BLOCK]
        eq_s[r] = jnp.exp(column).reshape(2, 2, ROWS, HEAD_DIM)
        ek_s[r] = jnp.exp(end - column)
        for half in range(2):
            at = half * HEAD_DIM
            gaps = jnp.minimum(column - row[:, at : at + HEAD_DIM], 0.0)
            i = lax.broadcasted_iota(jnp.int32, (BLOCK, HEAD_DIM), 0)
            k = lax.broadcasted_iota(jnp.int32, (BLOCK, HEAD_DIM), 1) + at
            mask_s[r, :, at : at + HEAD_DIM] = jnp.where(i >= k, jnp.exp(gaps), 0.0)

    for j in range(N_IN + 1):
        if j < N_IN:
            pass_near(j)
        for r in range(2 * HEADS):
            if r * (N_IN + 1) // (2 * HEADS) == j:
                decay_tables(r)
        if j == N_IN:
            for k in range(EARLY):
                pass_opposite(k)
        if j > 0:
            multiply_near(j - 1)

    def decay_size():
        return remote(
            dec.at[pl.ds(0, n_in - 1)], dec.at[pl.ds(0, n_in - 1)],
            dec_send, dec_recv, {"tensor": sib},
        )

    decay_size().wait_recv()
    my_head = place * chunk_rows // HEAD_DIM
    for i in range(n_in):
        edec[i : i + 1, :] = jnp.exp(dec[i, pl.ds(my_head, 1), :])

    for j in range(EARLY, N_IN + EARLY):
        if j < N_IN:
            pass_opposite(j)
        multiply_opposite(j - EARLY)
    remote(
        wo_ref, w2.at[pl.ds(HEADS * HEAD_DIM, HEADS * HEAD_DIM)],
        wo_send, wo_recv, {"tensor": sib},
    ).start()

    for h in range(HEADS):
        lanes = slice(h * HEAD_DIM, (h + 1) * HEAD_DIM)
        states = []
        for n in range(2):
            rows = slice(n * BLOCK, (n + 1) * BLOCK)
            keys = silu(block_of(1, n, lanes)).astype(BF16)
            values = block_of(2, n, lanes).astype(BF16)
            k_s[h, rows] = keys
            v_s[h, rows] = values
            weighted = (keys.astype(F32) * ek_s[n * HEADS + h]).astype(BF16)
            states.append(
                lax.dot_general(
                    weighted, values, (((0,), (0,)), ((), ())), preferred_element_type=F32
                )
            )
        u_s[h] = states[0]
        total = elast_s[HEADS + h : HEADS + h + 1, :] * states[0] + states[1]
        pieces = HEAD_DIM // chunk_rows
        st1[h * pieces : (h + 1) * pieces] = total.astype(BF16).reshape(
            pieces, chunk_rows, HEAD_DIM
        )

    for to in peers:
        remote(
            st1.at[to], rc1.at[place], p1_send, p1_recv, {"context": first + to}
        ).start()
    rc1[pl.ds(place, 1)] = st1[pl.ds(place, 1)]

    for j in range(N_IN):
        multiply(j, (OPPOSITE, 1), (0,))

    def attend(n):
        for h in range(HEADS):
            lanes = slice(h * HEAD_DIM, (h + 1) * HEAD_DIM)
            rows = slice(n * BLOCK, (n + 1) * BLOCK)
            queries = silu(block_of(0, n, lanes)).astype(BF16)
            weights = lax.dot_general(
                queries, k_s[h, rows, :], (((1,), (1,)), ((), ())), preferred_element_type=F32
            )
            weights = (weights * mask_s[n * HEADS + h]).astype(BF16)
            inner_s[h, 2 * n : 2 * n + 2] = jnp.dot(
                weights, v_s[h, rows, :], preferred_element_type=F32
            ).reshape(2, 2, ROWS, HEAD_DIM)
            scaled = queries.astype(F32).reshape(2, 2, ROWS, HEAD_DIM) * eq_s[n * HEADS + h]
            qs_s[h, 2 * n : 2 * n + 2] = scaled.astype(BF16)

    attend(0)

    def state_size(buffer, send, recv):
        others_of = buffer.at[pl.ds(0, n_in - 1)]
        return remote(others_of, others_of, send, recv, {"tensor": sib})

    state_size(rc1, p1_send, p1_recv).wait_recv()
    def group_copy(to):
        return remote(
            after, before.at[group], group_send.at[to], group_recv.at[group],
            {"context": to * n_in + place},
        )

    running = jnp.zeros((chunk_rows, HEAD_DIM), F32)
    kept = jnp.ones((16, HEAD_DIM), F32)
    for i in range(n_in):
        running = running * edec[i : i + 1, :] + rc1[i].astype(F32)
        kept = kept * edec[i : i + 1, :]
    after[0:chunk_rows] = running.astype(BF16)
    after[chunk_rows:] = two_parts(kept)
    for later_group in range(1, GROUPS):
        @pl.when(later_group > group)
        def _():
            pl.semaphore_wait(ready.at[later_group], 1)
            group_copy(later_group).start()

    running = jnp.zeros((chunk_rows, HEAD_DIM), F32)
    for earlier in range(GROUPS - 1):
        @pl.when(earlier < group)
        def _():
            remote(
                before.at[earlier], before.at[earlier], group_send.at[0],
                group_recv.at[earlier], {"tensor": sib},
            ).wait_recv()

        parts = before[earlier, chunk_rows:].astype(F32)
        running = running * (parts[0:1] + parts[8:9]) + before[earlier, 0:chunk_rows].astype(F32)
    for i in range(n_in):
        st2[i] = running.astype(BF16)
        running = running * edec[i : i + 1, :] + rc1[i].astype(F32)
    for to in peers:
        remote(
            st2.at[to], rc2.at[place], p2_send, p2_recv, {"context": first + to}
        ).start()
    rc2[pl.ds(place, 1)] = st2[pl.ds(place, 1)]

    attend(1)

    state_size(rc2, p2_send, p2_recv).wait_recv()

    pieces = HEAD_DIM // chunk_rows

    def normalize(which, target):
        for h in range(HEADS):
            lanes = slice(h * HEAD_DIM, (h + 1) * HEAD_DIM)
            entering = rc2[h * pieces : (h + 1) * pieces].reshape(HEAD_DIM, HEAD_DIM)
            later = elast_s[h : h + 1, :] * entering.astype(F32) + u_s[h]
            for n, state in enumerate((entering, later.astype(BF16))):
                queries = qs_s[h, 2 * n : 2 * n + 2, which].reshape(2 * ROWS, HEAD_DIM)
                attended = inner_s[h, 2 * n : 2 * n + 2, which].reshape(
                    2 * ROWS, HEAD_DIM
                ) + jnp.dot(queries, state, preferred_element_type=F32)
                size = jnp.mean(attended * attended, axis=1, keepdims=True)
                normed = (attended * lax.rsqrt(size + 1e-06)).astype(BF16)
                target[2 * n : 2 * n + 2, :, lanes] = normed.reshape(2, ROWS, HEAD_DIM)

    width = HEADS * HEAD_DIM
    normalize(other, nsend)
    norm_copy = remote(
        nsend, nrm.at[:, :, pl.ds(width, width)], n_send, n_recv, {"tensor": sib}
    )
    norm_copy.start()
    normalize(core, nrm)
    wo_copy.wait()
    w2_half = w2.at[pl.ds(width, width)]
    wo_wait = remote(w2_half, w2_half, wo_send, wo_recv, {"tensor": sib})
    wo_wait.wait_recv()
    norm_copy.wait_recv()

    def project(j):
        cols = out_cols(j)
        rows = nrm[...].reshape(N_Y * ROWS, 2 * width)
        chunk = jnp.dot(rows, w2[:, cols], preferred_element_type=F32).astype(BF16)
        part[:, :, cols] = chunk.reshape(N_Y, ROWS, nc)
        fwd, bwd = ring(j)
        remote(
            part.at[(y + 2) % N_Y, :, cols], relay.at[:, cols],
            rs_send, rs_relay.at[j], {"tensor": fwd * 2 + core},
        ).start()
        remote(
            part.at[bwd, :, cols], from_f.at[:, cols],
            rs_send, rs_f.at[j], {"tensor": bwd * 2 + core},
        ).start()

    def pass_on(j):
        cols = out_cols(j)
        fwd, _ = ring(j)
        remote(
            relay.at[:, cols], relay.at[:, cols], rs_send, rs_relay.at[j], {"tensor": sib}
        ).wait_recv()
        summed[:, cols] = (
            part[pl.ds(fwd, 1), :, cols].reshape(ROWS, nc).astype(F32)
            + relay[:, cols].astype(F32)
        ).astype(BF16)
        remote(
            summed.at[:, cols], from_b.at[:, cols],
            rs_sum_send, rs_b.at[j], {"tensor": fwd * 2 + core},
        ).start()

    def finish_rows(j):
        cols = out_cols(j)
        remote(
            from_f.at[:, cols], from_f.at[:, cols], rs_send, rs_f.at[j], {"tensor": sib}
        ).wait_recv()
        remote(
            from_b.at[:, cols], from_b.at[:, cols], rs_send, rs_b.at[j], {"tensor": sib}
        ).wait_recv()
        out_ref[:, cols] = (
            part[pl.ds(y, 1), :, cols].reshape(ROWS, nc).astype(F32)
            + from_f[:, cols].astype(F32)
            + from_b[:, cols].astype(F32)
        ).astype(out_ref.dtype)

    def project_step(j, carry):
        project(j)

        @pl.when(j >= LAG)
        def _():
            pass_on(j - LAG)

        return carry

    lax.fori_loop(0, OUT_CHUNKS, project_step, 0)

    def pass_step(j, carry):
        pass_on(j)
        finish_rows(j - (OUT_CHUNKS - LAG))
        return carry

    lax.fori_loop(OUT_CHUNKS - LAG, OUT_CHUNKS, pass_step, 0)

    seven = w2.at[pl.ds(0, 7 * ROWS)]
    remote(seven, seven, ag_send, ag_s.at[0], {"tensor": sib}).wait_send()
    wo_wait.wait_send()
    decay_size().wait_send()
    state_size(st1, p1_send, p1_recv).wait_send()
    state_size(st2, p2_send, p2_recv).wait_send()
    norm_copy.wait_send()

    for later_group in range(1, GROUPS):
        @pl.when(later_group > group)
        def _():
            group_copy(later_group).wait_send()


    def finish_step(j, carry):
        finish_rows(j)
        return carry

    lax.fori_loop(LAG, OUT_CHUNKS, finish_step, 0)
    two = part.at[pl.ds(0, 2)]
    remote(two, two, rs_send, rs_f.at[0], {"tensor": sib}).wait_send()
    remote(summed, summed, rs_sum_send, rs_b.at[0], {"tensor": sib}).wait_send()


def body(n_ctx, activations, w_qkv, w_out, log_decay):
    rows, d_model = activations.shape
    width = HEADS * HEAD_DIM
    n_in, chunk_rows = split(n_ctx)
    hbm = pl.BlockSpec(memory_space=pltpu.HBM)
    vmem = pl.BlockSpec(memory_space=pltpu.VMEM)
    dma = pltpu.SemaphoreType.DMA
    shard = N_TENSOR * rows
    scratch = [
        pltpu.VMEM((N_Y, 2, rows, d_model), BF16),
        pltpu.VMEM((3, d_model, width), BF16),
        pltpu.VMEM((2 * width, d_model), BF16),
        pltpu.VMEM((3, shard, width), F32),
        pltpu.VMEM((HEADS, N_Y, 2, rows, HEAD_DIM), BF16),
        pltpu.VMEM((HEADS, shard, HEAD_DIM), BF16),
        pltpu.VMEM((HEADS, shard, HEAD_DIM), BF16),
        pltpu.VMEM((2 * HEADS, BLOCK, BLOCK), F32),
        pltpu.VMEM((2 * HEADS, 2, 2, rows, HEAD_DIM), F32),
        pltpu.VMEM((2 * HEADS, BLOCK, HEAD_DIM), F32),
        pltpu.VMEM((HEADS, N_Y, 2, rows, HEAD_DIM), F32),
        pltpu.VMEM((HEADS, HEAD_DIM, HEAD_DIM), F32),
        pltpu.VMEM((HEADS, 2 * BLOCK), F32),
        pltpu.VMEM((2 * HEADS, BLOCK), F32),
        pltpu.VMEM((2 * HEADS, BLOCK), F32),
        pltpu.VMEM((2 * HEADS, HEAD_DIM), F32),
        pltpu.VMEM((2 * HEADS, HEAD_DIM), F32),
        pltpu.VMEM((n_in, 2 * HEADS, HEAD_DIM), F32),
        pltpu.VMEM((n_in, HEAD_DIM), F32),
        pltpu.VMEM((n_in, chunk_rows, HEAD_DIM), BF16),
        pltpu.VMEM((n_in, chunk_rows, HEAD_DIM), BF16),
        pltpu.VMEM((n_in, chunk_rows, HEAD_DIM), BF16),
        pltpu.VMEM((n_in, chunk_rows, HEAD_DIM), BF16),
        pltpu.VMEM((GROUPS - 1, chunk_rows + 16, HEAD_DIM), BF16),
        pltpu.VMEM((chunk_rows + 16, HEAD_DIM), BF16),
        pltpu.VMEM((N_Y, rows, width), BF16),
        pltpu.VMEM((N_Y, rows, 2 * width), BF16),
        pltpu.VMEM((N_Y, rows, d_model), BF16),
        pltpu.VMEM((rows, d_model), BF16),
        pltpu.VMEM((rows, d_model), BF16),
        pltpu.VMEM((rows, d_model), BF16),
        pltpu.VMEM((rows, d_model), BF16),
        dma,
        dma((N_IN,)),
        dma((N_IN,)),
        dma((N_IN,)),
        dma((N_IN,)),
        dma((N_IN,)),
        dma((N_IN,)),
        dma((N_IN,)),
        dma,
        dma,
        dma,
        dma,
        dma,
        dma,
        dma,
        dma,
        dma,
        dma,
        dma,
        dma,
        dma((OUT_CHUNKS,)),
        dma((OUT_CHUNKS,)),
        dma((OUT_CHUNKS,)),
        dma,
        dma,
        dma((GROUPS,)),
        dma((GROUPS,)),
        pltpu.SemaphoreType.REGULAR((GROUPS,)),
    ]
    return pl.pallas_call(
        functools.partial(kernel, n_ctx),
        out_shape=jax.ShapeDtypeStruct((rows, d_model), BF16),
        in_specs=[hbm, hbm, hbm, hbm],
        out_specs=vmem,
        scratch_shapes=scratch,
        compiler_params=pltpu.CompilerParams(
            collective_id=0, has_side_effects=True, vmem_limit_bytes=52 * 1024 * 1024
        ),
    )(*(
        pltpu.with_memory_space_constraint(array, pltpu.HBM)
        for array in (activations, w_qkv.transpose(1, 0, 2), w_out, log_decay)
    ))


def solution(mesh):
    in_specs = (
        P(("context", "tensor"), None),
        P(None, None, "tensor"),
        P("tensor", None),
        P("tensor", "context"),
    )
    out_specs = P(("context", "tensor"), None)
    return jax.shard_map(
        functools.partial(body, mesh.shape["context"]),
        mesh=mesh, in_specs=in_specs, out_specs=out_specs, check_vma=False,
    )
```
